128 devices in a mesh: ph: 16 (over y, x_lo, core), el: 8 (over x_hi, z).
Axes of the slice: x: 4 (x_hi: 2, x_lo: 2; x = x_hi * 2 + x_lo), y: 4, z: 4, core: 2. Of those that a mesh axis runs over, the one named last changes fastest.
Arguments:
- wannier_g: bfloat16 [128, 1024, 4, 2, 1024], P('el', 'ph'), may hold values from -0.078125 to 0.078125
- el_vectors: int32 [3, 128], P(None, 'el'), may hold values from -6 to 6
- ph_vectors: int32 [3, 1024], P(None, 'ph'), may hold values from -6 to 6
- el_degen: int32 [128], P('el'), may hold values from 1 to 8
- ph_degen: int32 [1024], P('ph'), may hold values from 1 to 8
- k_points: float32 [3, 16], replicated, may hold values from 0 to 1
- q_points: float32 [3, 128], replicated, may hold values from 0 to 1
- rot_right: float32 [16, 2, 32, 32], P('el'), may hold values from -0.75 to 0.75
- rot_left: float32 [16, 128, 2, 32, 32], P('el', 'ph'), may hold values from -0.75 to 0.75
Outputs:
- bloch_g: float32 [16, 128, 4, 2, 1024], P('el', 'ph')
The draws below stay inside these ranges and needn't reach their ends.
All inputs are finite; a program needn't handle non-finite values.
Results may differ from the reference program's by a relative error of at most 0.0034.
Values sent between devices are 32-bit elements; how exact they have to be, the bound alone decides.
No kernel may reach another device: no remote copies, remote signals or barrier semaphores. Data moves between devices by JAX's collectives and lax.ppermute only.
A program may use at most 448 MiB of HBM per device.

```python
import jax
import jax.numpy as jnp
from jax import lax

NW = 32
MODES = 4
RE = 128
RP = 1024
NK = 16
NQ = 128


def place_ends(drawn, stream_key, low, top_value):
    longest = drawn.shape.index(max(drawn.shape))
    spots = []
    for shift in (0, 1):
        where = [jax.random.randint(jax.random.fold_in(stream_key, axis), (), 0, length) for axis, length in enumerate(drawn.shape)]
        where[longest] = (where[longest] + shift) % drawn.shape[longest]
        spots.append(tuple(where))
    return drawn.at[spots[0]].set(low).at[spots[1]].set(top_value)


def levels(rng, dims, shards, low, top_value):
    level = 1.0
    for dim, shards_of in shards:
        heights = jax.random.uniform(jax.random.fold_in(jax.random.fold_in(rng, 6), dim), (shards_of,), jnp.float32, low / len(shards), top_value / len(shards))
        level = level * jnp.repeat(jnp.exp(heights), dims[dim] // shards_of).reshape((-1,) + (1,) * (len(dims) - 1 - dim))
    return level


def normal_values(key, extent, spread, bound, cuts=(), kind=jnp.bfloat16):
    array = spread * jax.random.normal(key, extent, jnp.float32)
    if cuts:
        array = array * levels(key, extent, cuts, -0.22, 0.18)
    return jnp.clip(array, -bound, bound).astype(kind)


def setup_inputs(seed: int = 0) -> dict:
    streams_of = jax.random.split(jax.random.key(seed), 10)
    return {
        "wannier_g": normal_values(streams_of[0], (RE, RP, MODES, 2, NW * NW), (2.0 / (RE * RP) ** 0.5), 0.078125, ((0, 8), (1, 16))),
        "el_vectors": place_ends(jax.random.randint(streams_of[1], (3, RE), -6, 7), jax.random.fold_in(streams_of[1], 1), -6, 6).astype(jnp.int32),
        "ph_vectors": place_ends(jax.random.randint(streams_of[2], (3, RP), -6, 7), jax.random.fold_in(streams_of[2], 1), -6, 6).astype(jnp.int32),
        "el_degen": place_ends(jax.random.randint(streams_of[3], (RE,), 1, 9), jax.random.fold_in(streams_of[3], 1), 1, 8).astype(jnp.int32),
        "ph_degen": place_ends(jax.random.randint(streams_of[4], (RP,), 1, 9), jax.random.fold_in(streams_of[4], 1), 1, 8).astype(jnp.int32),
        "k_points": jnp.clip(jax.random.uniform(streams_of[5], (3, NK), jnp.float32, 0.0, 1.0), 0.0, 1.0),
        "q_points": jnp.clip(jax.random.uniform(streams_of[6], (3, NQ), jnp.float32, 0.0, 1.0), 0.0, 1.0),
        "rot_right": normal_values(streams_of[7], (NK, 2, NW, NW), (2 * NW) ** -0.5, 0.75, ((0, 8),), jnp.float32),
        "rot_left": normal_values(streams_of[8], (NK, NQ, 2, NW, NW), (2 * NW) ** -0.5, 0.75, ((0, 8), (1, 16)), jnp.float32),
    }


def phase_table(points, vectors, degen):
    coords = vectors.astype(jnp.float32)
    angle = points[0][:, None] * coords[0][None, :] + points[1][:, None] * coords[1][None, :]
    angle = angle + points[2][:, None] * coords[2][None, :]
    angle = 2.0 * jnp.pi * angle
    scale = 1.0 / degen.astype(jnp.float32)
    return (jnp.cos(angle) * scale[None, :]).astype(jnp.bfloat16), (jnp.sin(angle) * scale[None, :]).astype(jnp.bfloat16)


def combine(cos_part, sin_part):
    real_part = cos_part[..., 0, :] - sin_part[..., 1, :]
    imag_part = cos_part[..., 1, :] + sin_part[..., 0, :]
    return jnp.stack([real_part, imag_part], axis=-2)


def rotate(summed, rot_right, rot_left):
    nk, nq, modes = summed.shape[0], summed.shape[1], summed.shape[2]
    nw = rot_right.shape[-1]
    matrix = summed.reshape(nk, nq, modes, 2, nw, nw)
    g_real, g_imag = matrix[:, :, :, 0], matrix[:, :, :, 1]
    r_real, r_imag = rot_right[:, 0], rot_right[:, 1]
    l_real, l_imag = rot_left[:, :, 2 * 0], rot_left[:, :, 1]
    hp = lax.Precision.HIGHEST
    a_real = jnp.einsum('kqmab,kbc->kqmac', g_real, r_real, precision=hp) - jnp.einsum('kqmab,kbc->kqmac', g_imag, r_imag, precision=hp)
    a_imag = jnp.einsum('kqmab,kbc->kqmac', g_real, r_imag, precision=hp) + jnp.einsum('kqmab,kbc->kqmac', g_imag, r_real, precision=hp)
    o_real = jnp.einsum('kqai,kqmac->kqmic', l_real, a_real, precision=hp) + jnp.einsum('kqai,kqmac->kqmic', l_imag, a_imag, precision=hp)
    o_imag = jnp.einsum('kqai,kqmac->kqmic', l_real, a_imag, precision=hp) - jnp.einsum('kqai,kqmac->kqmic', l_imag, a_real, precision=hp)
    return jnp.stack([o_real, o_imag], axis=3).reshape(nk, nq, modes, 2, nw * nw)


def reference(wannier_g, el_vectors, ph_vectors, el_degen, ph_degen, k_points, q_points, rot_right, rot_left):
    q_cos, q_sin = phase_table(q_points, ph_vectors, ph_degen)
    k_cos, k_sin = phase_table(k_points, el_vectors, el_degen)
    flat = wannier_g.reshape(RE, RP, MODES * 2 * NW * NW)

    def one_row(rows):
        return (jnp.dot(q_cos, rows, preferred_element_type=jnp.float32),
                jnp.dot(q_sin, rows, preferred_element_type=jnp.float32))

    cos_part, sin_part = lax.map(one_row, flat)
    mixed = combine(cos_part.reshape(RE, NQ, MODES, 2, NW * NW), sin_part.reshape(RE, NQ, MODES, 2, NW * NW))
    mixed = mixed.reshape(RE, NQ * MODES * 2 * NW * NW)
    hp = lax.Precision.HIGHEST
    kc = k_cos.astype(jnp.float32)
    ks = k_sin.astype(jnp.float32)
    cos_two = jnp.dot(kc, mixed, precision=hp).reshape(NK, NQ, MODES, 2, NW * NW)
    sin_two = jnp.dot(ks, mixed, precision=hp).reshape(NK, NQ, MODES, 2, NW * NW)
    summed = combine(cos_two, sin_two)
    return rotate(summed, rot_right, rot_left)
```

```python
import jax
import jax.numpy as jnp
from jax import lax
from jax.experimental import pallas as pl
from jax.experimental.pallas import tpu as pltpu
from jax.sharding import Mesh, PartitionSpec as P

LANES = 256
PARTS = {"z": (0, 1, 2), "x": (3, 4, 5), "y": (6, 7)}
ORDER = {"z": ("z", "x", "y"), "x": ("x", "y", "z"), "y": ("y", "z", "x")}
DIMS = ("xh", "z", "i", "y", "xl", "c", "u", "m", "j", "w")
SIZES = {"xh": 2, "z": 4, "i": 2, "y": 4, "xl": 2, "c": 2}


def phase_table(points, coords, degen):
    angle = points[0][:, None] * coords[0][None, :] + points[1][:, None] * coords[1][None, :]
    angle = angle + points[2][:, None] * coords[2][None, :]
    angle = 2.0 * jnp.pi * angle
    scale = 1.0 / degen
    return (
        (jnp.cos(angle) * scale[None, :]).astype(jnp.bfloat16),
        (jnp.sin(angle) * scale[None, :]).astype(jnp.bfloat16),
    )


def partial_kernel(wq_ref, wk_ref, own_ref, got_ref, out_ref, mixed_ref):
    for r in range(16):
        own = own_ref[r, 0]
        got = got_ref[r, 0].astype(jnp.bfloat16)
        rows = jnp.concatenate([own[0], got[0], own[1], got[1]], axis=0)
        mixed = jnp.dot(wq_ref[...], rows, preferred_element_type=jnp.float32)
        mixed_ref[:, r] = mixed.reshape(2, 16, 8, LANES)
    for g in range(16):
        rows = mixed_ref[:, :, g].reshape(256, LANES).astype(jnp.bfloat16)
        summed = jnp.dot(wk_ref[...], rows, preferred_element_type=jnp.float32)
        out_ref[:, g, 0] = summed.reshape(16, 2, 8, LANES)


def partial_sums(wq, wk, own, got, first, count):
    return pl.pallas_call(
        partial_kernel,
        grid=(count,),
        in_specs=[
            pl.BlockSpec((256, 256), lambda u: (0, 0)),
            pl.BlockSpec((256, 256), lambda u: (0, 0)),
            pl.BlockSpec((16, 1, 2, 64, LANES), lambda u: (0, (u + first) // 4, 0, 0, (u + first) % 4)),
            pl.BlockSpec((16, 1, 2, 64, LANES), lambda u: (0, (u + first) // 4, 0, 0, (u + first) % 4)),
        ],
        out_specs=pl.BlockSpec((16, 16, 1, 2, 8, LANES), lambda u: (0, 0, u, 0, 0, 0)),
        out_shape=jax.ShapeDtypeStruct((16, 16, count, 2, 8, LANES), jnp.float32),
        scratch_shapes=[pltpu.VMEM((2, 16, 16, 8, LANES), jnp.float32)],
        compiler_params=pltpu.CompilerParams(vmem_limit_bytes=48 * 1024 * 1024),
        cost_estimate=pl.CostEstimate(
            flops=2 * 2 * 16 * 256 * 256 * LANES * count,
            bytes_accessed=count * LANES * (16 * 128 * 6 + 256 * 16 * 4),
            transcendentals=0,
        ),
    )(wq, wk, own, got)


def chunk(array, dims, axis, place):
    cuts = {"x": (("xh", place // 2), ("xl", place % 2))}.get(axis, ((axis, place),))
    starts = [0] * len(dims)
    sizes = list(array.shape)
    left = list(dims)
    for name, at in cuts:
        spot = dims.index(name)
        starts[spot], sizes[spot] = at, 1
        left.remove(name)
    piece = lax.dynamic_slice(array, starts, sizes)
    return piece.reshape([n for n, d in zip(sizes, dims) if d in left]), tuple(left)


def ring_pairs(axis):
    pairs = []
    for core in range(2):
        for at in range(4):
            to = (at + 1 - 2 * core) % 4
            if axis == "z":
                pairs.append((core * 4 + at, core * 4 + to))
            elif axis == "y":
                pairs.append((at * 2 + core, to * 2 + core))
            else:
                pairs.append(((at % 2) * 4 + core * 2 + at // 2, (to % 2) * 4 + core * 2 + to // 2))
    return pairs


RING_AXES = {"z": ("c", "z"), "y": ("y", "c"), "x": ("xl", "c", "xh")}


def rotate(summed, rot_right, rot_left):
    nk, nq, modes = (summed.shape[0], summed.shape[1], summed.shape[2])
    nw = rot_right.shape[-1]
    matrix = summed.reshape(nk, nq, modes, 2, nw, nw)
    g_real, g_imag = (matrix[:, :, :, 0], matrix[:, :, :, 1])
    r_real, r_imag = (rot_right[:, 0], rot_right[:, 1])
    l_real, l_imag = (rot_left[:, :, 0], rot_left[:, :, 1])
    hp = lax.Precision.HIGHEST
    a_real = jnp.einsum("kqmab,kbc->kqmac", g_real, r_real, precision=hp) - jnp.einsum(
        "kqmab,kbc->kqmac", g_imag, r_imag, precision=hp
    )
    a_imag = jnp.einsum("kqmab,kbc->kqmac", g_real, r_imag, precision=hp) + jnp.einsum(
        "kqmab,kbc->kqmac", g_imag, r_real, precision=hp
    )
    o_real = jnp.einsum("kqai,kqmac->kqmic", l_real, a_real, precision=hp) + jnp.einsum(
        "kqai,kqmac->kqmic", l_imag, a_imag, precision=hp
    )
    o_imag = jnp.einsum("kqai,kqmac->kqmic", l_real, a_imag, precision=hp) - jnp.einsum(
        "kqai,kqmac->kqmic", l_imag, a_real, precision=hp
    )
    return jnp.stack([o_real, o_imag], axis=3).reshape(nk, nq, modes, 2, nw * nw)


def complex_table(cos_part, sin_part):
    top = jnp.concatenate([cos_part, -sin_part], axis=1)
    bottom = jnp.concatenate([sin_part, cos_part], axis=1)
    return jnp.concatenate([top, bottom], axis=0)


def body(
    wannier_g, el_vectors, ph_vectors, el_degen, ph_degen, k_points, q_points, rot_right, rot_left
):
    core = lax.axis_index("c")
    place = {
        "z": lax.axis_index("z"),
        "y": lax.axis_index("y"),
        "x": lax.axis_index("xh") * 2 + lax.axis_index("xl"),
    }
    step = 1 - 2 * core
    swap = lambda v: lax.ppermute(v, "c", [(0, 1), (1, 0)])

    sent = lax.dynamic_slice_in_dim(wannier_g, 2 - 2 * core, 2, axis=2)
    got = swap(sent.transpose(0, 2, 3, 1, 4).astype(jnp.float32))
    own = lax.dynamic_slice_in_dim(wannier_g, 2 * core, 2, axis=2).transpose(0, 2, 3, 1, 4)

    vectors = jnp.concatenate([ph_vectors, ph_degen[None]], axis=0).astype(jnp.float32)
    vectors = jnp.concatenate([vectors, swap(vectors)], axis=1)
    wq = complex_table(*phase_table(q_points, vectors[:3], vectors[3]))
    k_cos, k_sin = phase_table(k_points, el_vectors.astype(jnp.float32), el_degen.astype(jnp.float32))
    wide = jnp.stack([jnp.stack([k_cos, -k_sin], 1), jnp.stack([k_sin, k_cos], 1)], 1)
    wk = wide.reshape(32, 1, 32, 1) * jnp.eye(8, dtype=jnp.bfloat16)[None, :, None, :]
    wk = wk.reshape(256, 256)

    held = {}
    for part, units in PARTS.items():
        sums = partial_sums(wq, wk, own, got, units[0], len(units))
        held[part] = (sums.reshape(2, 4, 2, 4, 2, 2, len(units), 2, 8, LANES), DIMS)
    for phase in range(3):
        running = {}
        for part in PARTS:
            axis = ORDER[part][phase]
            running[part] = chunk(*held[part], axis, (place[axis] - step) % 4)
        for hop in range(3):
            for part in PARTS:
                axis = ORDER[part][phase]
                arrived = lax.ppermute(running[part][0], RING_AXES[axis], ring_pairs(axis))
                mine, dims = chunk(*held[part], axis, (place[axis] - step * (hop + 2)) % 4)
                running[part] = (arrived + mine, dims)
        held = running

    done = jnp.concatenate([held[part][0] for part in PARTS], axis=2)
    mine = lax.dynamic_index_in_dim(done, core, axis=1, keepdims=False)
    other = swap(lax.dynamic_index_in_dim(done, 1 - core, axis=1, keepdims=False))
    modes = jnp.stack([jnp.where(core == 0, mine, other), jnp.where(core == 0, other, mine)], axis=1)
    modes = modes.reshape(2, 4, 4, 2, 8, LANES)
    summed = modes.transpose(0, 4, 1, 3, 2, 5).reshape(2, 8, 4, 2, 4 * LANES)
    return rotate(summed, rot_right, rot_left)


def solution(mesh):
    fine = Mesh(mesh.devices.reshape(4, 2, 2, 2, 4), ("y", "xl", "c", "xh", "z"))
    ph, el = ("y", "xl", "c"), ("xh", "z")
    in_specs = (
        P(el, ph, None, None, None),
        P(None, el),
        P(None, ph),
        P(el),
        P(ph),
        P(),
        P(),
        P(el, None, None, None),
        P(el, ph, None, None, None),
    )
    out_specs = P(el, ph, None, None, None)
    return jax.shard_map(body, mesh=fine, in_specs=in_specs, out_specs=out_specs, check_vma=False)
```

```python
import itertools
import math

import jax
import jax.numpy as jnp
from jax import lax
from jax.experimental import pallas as pl
from jax.experimental.pallas import tpu as pltpu
from jax.sharding import Mesh, PartitionSpec as P

FIRST = 384
BLOCK = 128
BLOCKS = 5
PAIRS = 3
ORDER = {"z": "zxy", "x": "xyz", "y": "yzx"}
EVENTS = (
    *("z0", "x0", "y0", "z1", "x1", "zk"),
    *("y1", "x2", "z2", "y2", "x3", "z3"),
    *("y3", "z4", "x4", "y4", "z5", "x5", "y5"),
)


def block_place(part, t):
    if part == "x":
        return t // 3, t + 3
    return (t + 1) // 3, jnp.where(t < 2, t + 6, t + 1)


def phase_table(points, coords, degen):
    angle = points[0][:, None] * coords[0][None, :] + points[1][:, None] * coords[1][None, :]
    angle = angle + points[2][:, None] * coords[2][None, :]
    angle = 2.0 * jnp.pi * angle
    scale = 1.0 / degen
    return (
        (jnp.cos(angle) * scale[None, :]).astype(jnp.bfloat16),
        (jnp.sin(angle) * scale[None, :]).astype(jnp.bfloat16),
    )


def ring_place(place, core, first, second):
    high = place >> 1
    low = high ^ (place & 1)
    low = low ^ jnp.where(core == 0, first, second)
    high = high ^ jnp.where(core == 0, second, first)
    return 2 * high + (low ^ high)


def widen_kernel(where_ref, own_ref, out_ref):
    out_ref[...] = own_ref[:, 0].astype(jnp.float32)


def spread(table_ref, wide_ref):
    rows = lax.broadcasted_iota(jnp.int32, (256, 32), 0)
    entry = lax.broadcasted_iota(jnp.int32, (256, 32), 1)
    pick = (rows // 8 == entry).astype(jnp.float32).astype(jnp.bfloat16)
    table = jnp.dot(pick, table_ref[...], preferred_element_type=jnp.float32).astype(jnp.bfloat16)
    table = lax.dot_general(table, pick, (((1,), (1,)), ((), ())), preferred_element_type=jnp.float32)
    rows = lax.broadcasted_iota(jnp.int32, (256, 256), 0)
    entry = lax.broadcasted_iota(jnp.int32, (256, 256), 1)
    table = jnp.where(rows % 8 == entry % 8, table, 0.0).astype(jnp.bfloat16)
    wide_ref[...] = table.reshape(8, 32, 256)


def partial_kernel(order, where_ref, wq_ref, wk_ref, even_ref, odd_ref, got_ref, *refs):
    *out_refs, mixed_ref, rows_ref, wide_ref = refs
    core, y, z, xh, xl = (where_ref[n] for n in range(5))
    lanes = got_ref.shape[-1]

    @pl.when(pl.program_id(0) == 0)
    def _():
        spread(wk_ref, wide_ref)
        for h, zf, zs in itertools.product(range(2), repeat=3):
            zat = ring_place(z, core, zf, zs)
            spot = 32 * (4 * h + 2 * zf + zs)
            rows_ref[0, spot : spot + 32] = wide_ref[(xh ^ h) * 4 + zat]
            rows_ref[1, spot : spot + 32] = wide_ref[(xh ^ h ^ core) * 4 + zat]

    for r in range(16):
        even = even_ref[r, 0].reshape(128, BLOCK)
        odd = odd_ref[r, 0].reshape(128, BLOCK)
        own = jnp.concatenate([even, odd], axis=1)
        got = got_ref[r].reshape(128, lanes).astype(jnp.bfloat16)
        rows = jnp.concatenate([own, got], axis=0)
        mixed = jnp.dot(wq_ref[...], rows, preferred_element_type=jnp.float32)
        mixed_ref[r] = mixed.reshape(2, 16, 8, lanes)
    for yf, ys, cross, other in itertools.product(range(2), repeat=4):
        g = ring_place(y, core, yf, ys) * 4 + (xl ^ cross) * 2 + (core ^ other)
        rows = mixed_ref[:, :, g].reshape(256, lanes).astype(jnp.bfloat16)
        summed = jnp.dot(rows_ref[cross], rows, preferred_element_type=jnp.float32)
        summed = summed.reshape(2, 2, 2, 2, 2, 8, lanes)
        for h, zf, zs in itertools.product(range(2), repeat=3):
            bits = {"y": (yf, ys), "z": (zf, zs), "x": (h ^ cross, h)}
            spot = sum((bits[axis] for axis in order), ())
            out_refs[spot[0]][(*spot[1:], other)] = summed[h, zf, zs]


def electron_kernel(where_ref, wk_ref, own_ref, *refs):
    *out_refs, rows_ref, wide_ref = refs
    core, z, xh = (where_ref[n] for n in (0, 2, 3))
    lanes = own_ref.shape[-1]

    @pl.when(pl.program_id(0) == 0)
    def _():
        spread(wk_ref, wide_ref)
        for zf, zs, h in itertools.product(range(2), repeat=3):
            spot = 32 * (4 * zf + 2 * zs + h)
            rows_ref[spot : spot + 32] = wide_ref[(xh ^ h) * 4 + ring_place(z, core, zf, zs)]

    for pair in range(4):
        wide = own_ref[:, 0, :, 16 * pair : 16 * pair + 16].astype(jnp.float32)
        for half in range(2):
            rows = wide[:, :, 8 * half : 8 * half + 8].reshape(256, lanes).astype(jnp.bfloat16)
            summed = jnp.dot(rows_ref[...], rows, preferred_element_type=jnp.float32)
            summed = summed.reshape(2, 2, 2, 2, 2, 8, lanes)
            for n in range(2):
                out_refs[n][:, 0, :, :, 2 * pair + half, 0] = summed[n]


def phonon_kernel(where_ref, wq_ref, own_ref, got_ref, keep_ref, send_ref, summed_ref):
    core, y, xl = (where_ref[n] for n in (0, 1, 4))
    lanes = own_ref.shape[-1]
    for h, i in itertools.product(range(2), repeat=2):
        rows = [jnp.swapaxes(ref[h, i, :, 0], 0, 1).reshape(128, lanes) for ref in (own_ref, got_ref)]
        rows = jnp.concatenate(rows, axis=0).astype(jnp.bfloat16)
        summed = jnp.dot(wq_ref[...], rows, preferred_element_type=jnp.float32)
        summed_ref[h, i] = summed.reshape(2, 16, 8, lanes)
    for xf, xs in itertools.product(range(2), repeat=2):
        h = jnp.where(core == 0, xs, xf)
        for yf, ys, other in itertools.product(range(2), repeat=3):
            g = ring_place(y, core, yf, ys) * 4 + (xl ^ xf ^ xs) * 2 + (core ^ other)
            for i in range(2):
                (keep_ref, send_ref)[xf][xs, yf, ys, other, i, 0] = summed_ref[h, i, :, g]


def kernel_call(kernel, where, inputs, in_specs, count, out, block, place, grid, scratch):
    read = sum(v.size * v.dtype.itemsize for v in inputs)
    return pl.pallas_call(
        kernel,
        grid_spec=pltpu.PrefetchScalarGridSpec(
            num_scalar_prefetch=1,
            grid=(grid,),
            in_specs=in_specs,
            out_specs=[pl.BlockSpec(block, place)] * count,
            scratch_shapes=scratch,
        ),
        out_shape=[jax.ShapeDtypeStruct(out, jnp.float32)] * count,
        compiler_params=pltpu.CompilerParams(vmem_limit_bytes=48 * 1024 * 1024),
        cost_estimate=pl.CostEstimate(
            flops=2**31, bytes_accessed=read + 4 * count * math.prod(out), transcendentals=0
        ),
    )(where, *inputs)


def electron_sums(where, wk, own):
    return kernel_call(
        electron_kernel,
        where,
        (wk, own),
        [
            pl.BlockSpec((32, 32), lambda m, w: (0, 0)),
            pl.BlockSpec((16, 1, 2, 64, FIRST), lambda m, w: (0, (2 * w[0] + m) % 4, 0, 0, 0)),
        ],
        2,
        (2, 2, 2, 2, 8, 2, 2, 8, FIRST),
        (2, 1, 2, 2, 8, 1, 2, 8, FIRST),
        lambda m, w: (0, m // 2, 0, 0, 0, m % 2, 0, 0, 0),
        4,
        [pltpu.VMEM((256, 256), jnp.bfloat16), pltpu.VMEM((8, 32, 256), jnp.bfloat16)],
    )


def phonon_sums(where, wq, own, got):
    spec = pl.BlockSpec((2, 2, 8, 1, 2, 8, FIRST), lambda u, w: (0, 0, 0, u, 0, 0, 0))
    return kernel_call(
        phonon_kernel,
        where,
        (wq, own, got),
        [pl.BlockSpec((256, 256), lambda u, w: (0, 0)), spec, spec],
        2,
        (2, 2, 2, 2, 2, 2, 2, 8, FIRST),
        (2, 2, 2, 2, 2, 1, 2, 8, FIRST),
        lambda u, w: (0, 0, 0, 0, 0, u, 0, 0, 0),
        2,
        [pltpu.VMEM((2, 2, 2, 16, 8, FIRST), jnp.float32)],
    )


def own_spec(part, flip, block_of):
    def place(t, w):
        mode, block = block_place(part, block_of(t))
        return (0, 2 * (w[0] ^ flip) + mode, 0, 0, block)

    return pl.BlockSpec((16, 1, 2, 64, BLOCK), place)


def widened(part, where, own):
    return kernel_call(
        widen_kernel,
        where,
        (own,),
        [own_spec(part, 1, lambda t: t)],
        1,
        (16, 2, 64, BLOCKS * BLOCK),
        (16, 2, 64, BLOCK),
        lambda t, w: (0, 0, 0, t),
        BLOCKS,
        [],
    )[0]


def partial_sums(part, where, wq, wk, own, got):
    return kernel_call(
        lambda *refs: partial_kernel(ORDER[part], *refs),
        where,
        (wq, wk, own, own, got),
        [
            pl.BlockSpec((256, 256), lambda t, w: (0, 0)),
            pl.BlockSpec((32, 32), lambda t, w: (0, 0)),
            own_spec(part, 0, lambda t: 2 * t),
            own_spec(part, 0, lambda t: jnp.minimum(2 * t + 1, BLOCKS - 1)),
            pl.BlockSpec((16, 2, 64, 2 * BLOCK), lambda t, w: (0, 0, 0, t)),
        ],
        2,
        (2, 2, 2, 2, 2, 2, 2, 2, 8, BLOCKS * BLOCK),
        (2, 2, 2, 2, 2, 2, 2, 2, 8, 2 * BLOCK),
        lambda t, w: (0, 0, 0, 0, 0, 0, 0, 0, 0, t),
        PAIRS,
        [
            pltpu.VMEM((16, 2, 16, 8, 2 * BLOCK), jnp.float32),
            pltpu.VMEM((2, 256, 256), jnp.bfloat16),
            pltpu.VMEM((8, 32, 256), jnp.bfloat16),
        ],
    )


def exchange(value, axis, step):
    pairs = []
    for core in range(2):
        for at in range(4):
            to = at ^ 1 if core == step else 3 - at
            if axis == "z":
                pairs.append((core * 4 + at, core * 4 + to))
            elif axis == "y":
                pairs.append((at * 2 + core, to * 2 + core))
            else:
                pairs.append(((at % 2) * 4 + core * 2 + at // 2, (to % 2) * 4 + core * 2 + to // 2))
    names = {"z": ("c", "z"), "y": ("y", "c"), "x": ("xl", "c", "xh")}[axis]
    return lax.ppermute(value, names, pairs)


def swap(value):
    return lax.ppermute(value, "c", [(0, 1), (1, 0)])


def rotation_tables(rot_right, rot_left):
    r_real, r_imag = (rot_right[:, 0], rot_right[:, 1])
    l_real, l_imag = (rot_left[:, :, 0], rot_left[:, :, 1])
    right = jnp.stack([jnp.stack([r_real, r_imag], 2), jnp.stack([-r_imag, r_real], 2)], 1)
    left = jnp.stack([jnp.stack([l_real, -l_imag], 3), jnp.stack([l_imag, l_real], 3)], 2)
    right = right.transpose(0, 1, 3, 2, 4)[:, :, :, None, :, None, :]
    right = right * jnp.eye(8, dtype=jnp.float32)[:, None, :, None]
    left = left.transpose(0, 1, 4, 5, 2, 3)
    return right.reshape(2, 2, 2, 256, 256), left.reshape(2, 8, 64, 64)


def split(value):
    high = value.astype(jnp.bfloat16)
    return high, (value - high.astype(jnp.float32)).astype(jnp.bfloat16)


def dot(left, right):
    return jnp.dot(left, right, preferred_element_type=jnp.float32)


def regroup(parts):
    group = lax.broadcasted_iota(jnp.int32, (8, 128), 1) // 32
    out = []
    for n in range(4):
        total = parts[n]
        for m in range(4):
            if m != n:
                total = jnp.where(group == m, pltpu.roll(parts[m], 32 * (m - n) % 128, 1), total)
        out.append(total)
    return out


def rotation_kernel(sum_ref, right_ref, left_ref, out_ref, turned_ref, done_ref):
    turned = [0.0, 0.0]
    for p in range(2):
        rows = sum_ref[0, p].reshape(32, 1024)
        rows = jnp.concatenate([rows[:, 256 * t : 256 * t + 256] for t in range(4)], axis=0)
        high, low = split(rows)
        both = jnp.concatenate([high, low], axis=0)
        for s in range(2):
            right_high, right_low = split(right_ref[0, p, s])
            product = dot(both, right_high)
            turned[s] = turned[s] + product[:128] + product[128:] + dot(high, right_low)
    for s in range(2):
        blocks = turned[s].reshape(4, 4, 8, 256)
        for t in range(8):
            parts = [blocks[t // 2, m, :, 128 * (t % 2) : 128 * (t % 2) + 128] for m in range(4)]
            for n, part in enumerate(regroup(parts)):
                spot = 8 * (32 * s + 4 * t + n)
                turned_ref[spot : spot + 8] = part
    for j in range(8):
        high, low = split(turned_ref[pl.ds(j, 64, stride=8), :])
        left_high, left_low = split(left_ref[0, j])
        product = dot(jnp.concatenate([left_high, left_low], axis=0), high)
        done_ref[pl.ds(j, 64, stride=8), :] = product[:64] + product[64:] + dot(left_high, low)
    for s in range(2):
        for t in range(8):
            spot = 8 * (32 * s + 4 * t)
            parts = [done_ref[spot + 8 * n : spot + 8 * n + 8] for n in range(4)]
            for m, part in enumerate(regroup(parts)):
                out_ref[0, :, m, s, 128 * t : 128 * t + 128] = part


def rotate(summed, right, left):
    return pl.pallas_call(
        rotation_kernel,
        grid=(2,),
        in_specs=[
            pl.BlockSpec((1, 2, 4, 8, 1024), lambda k: (k, 0, 0, 0, 0)),
            pl.BlockSpec((1, 2, 2, 256, 256), lambda k: (k, 0, 0, 0, 0)),
            pl.BlockSpec((1, 8, 64, 64), lambda k: (k, 0, 0, 0)),
        ],
        out_specs=pl.BlockSpec((1, 8, 4, 2, 1024), lambda k: (k, 0, 0, 0, 0)),
        out_shape=jax.ShapeDtypeStruct((2, 8, 4, 2, 1024), jnp.float32),
        scratch_shapes=[pltpu.VMEM((512, 128), jnp.float32)] * 2,
        compiler_params=pltpu.CompilerParams(vmem_limit_bytes=48 * 1024 * 1024),
        cost_estimate=pl.CostEstimate(flops=2**28, bytes_accessed=2**22, transcendentals=0),
    )(summed, right, left)


def complex_table(cos_part, sin_part):
    top = jnp.concatenate([cos_part, -sin_part], axis=1)
    bottom = jnp.concatenate([sin_part, cos_part], axis=1)
    return jnp.concatenate([top, bottom], axis=0)


def body(
    wannier_g, el_vectors, ph_vectors, el_degen, ph_degen, k_points, q_points, rot_right, rot_left
):
    core = lax.axis_index("c")
    where = jnp.stack([core, *(lax.axis_index(a) for a in ("y", "z", "xh", "xl"))]).astype(jnp.int32)

    vectors = jnp.concatenate([ph_vectors, ph_degen[None]], axis=0).astype(jnp.float32)
    others = swap(vectors)
    k_cos, k_sin = phase_table(k_points, el_vectors.astype(jnp.float32), el_degen.astype(jnp.float32))
    wide = jnp.stack([jnp.stack([k_cos, -k_sin], 2), jnp.stack([k_sin, k_cos], 2)], 1)
    wk = wide.reshape(32, 32)
    tables = [complex_table(*phase_table(q_points, v[:3], v[3])) for v in (vectors, others)]
    wq = jnp.concatenate(tables, axis=1)

    own = lax.optimization_barrier(wannier_g.transpose(0, 2, 3, 1, 4))

    def after(earlier, *values):
        return lax.optimization_barrier((*values, earlier))[:-1]

    keep, send, arrived = {}, {}, {}

    def begin(part, sums):
        keep[part], send[part] = sums
        arrived[part] = exchange(send[part], part, 0)

    (own,) = after(others, own)
    got_x = widened("x", where, own)
    (wk,) = after(got_x, wk)
    got_x = swap(got_x)
    begin("z", electron_sums(where, wk, own))
    (later,) = after(keep["z"], own)
    got_y = widened("y", where, later)
    wq, got_x = after(got_y, wq, got_x)
    got_y = swap(got_y)
    begin("x", partial_sums("x", where, wq, wk, own, got_x))
    wq, got_y = after(keep["x"], wq, got_y)
    begin("y", partial_sums("y", where, wq, wk, own, got_y))
    rot_right, rot_left = after(keep["y"], rot_right, rot_left)
    right, left = rotation_tables(rot_right, rot_left)
    latest = (right, left, keep["y"])
    for event in EVENTS:
        part, step = event
        axes = ORDER[part]
        (arrived[part],) = after(latest, arrived[part])
        if step == "0":
            latest = send[part] = keep[part][1] + arrived[part][1]
            held, came = after(latest, keep[part], arrived[part])
            arrived[part] = exchange(send[part], axes[0], 1)
            keep[part] = held[0] + came[0]
        elif step == "k":
            keep[part], send[part] = phonon_sums(where, wq, keep[part], arrived[part])
            arrived[part] = exchange(send[part], axes[1], 0)
            latest = keep[part]
        elif step == "5":
            latest = keep[part] = keep[part] + arrived[part]
        else:
            latest = send[part] = keep[part][1] + arrived[part][1]
            keep[part] = keep[part][0] + arrived[part][0]
            if event == "z1":
                arrived[part] = swap(send[part])
            else:
                arrived[part] = exchange(send[part], axes[(int(step) + 1) // 2], (int(step) + 1) % 2)

    modes = []
    for ours in (True, False):
        z, x, y = (keep[part][0] if ours else swap(keep[part][1]) for part in "zxy")
        wide, narrow = 3 * BLOCK, 2 * BLOCK
        modes.append(jnp.concatenate([z[:, 0], x[..., :wide], y[..., :narrow]], axis=-1))
        modes.append(jnp.concatenate([z[:, 1], y[..., narrow:], x[..., wide:]], axis=-1))
    mine, theirs = jnp.stack(modes[:2], axis=2), jnp.stack(modes[2:], axis=2)
    modes = jnp.concatenate([jnp.where(core == 0, mine, theirs), jnp.where(core == 0, theirs, mine)], axis=2)
    return rotate(modes, right, left)


def solution(mesh):
    fine = Mesh(mesh.devices.reshape(4, 2, 2, 2, 4), ("y", "xl", "c", "xh", "z"))
    ph, el = ("y", "xl", "c"), ("xh", "z")
    in_specs = (
        P(el, ph, None, None, None),
        P(None, el),
        P(None, ph),
        P(el),
        P(ph),
        P(),
        P(),
        P(el, None, None, None),
        P(el, ph, None, None, None),
    )
    out_specs = P(el, ph, None, None, None)
    return jax.shard_map(body, mesh=fine, in_specs=in_specs, out_specs=out_specs, check_vma=False)
```

```python
import itertools
import math

import jax
import jax.numpy as jnp
from jax import lax
from jax.experimental import pallas as pl
from jax.experimental.pallas import tpu as pltpu
from jax.sharding import Mesh, PartitionSpec as P

FIRST = 384
BLOCK = 128
BLOCKS = 5
PAIRS = 3
ORDER = {"z": "zxy", "x": "xyz", "y": "yzx"}
EVENTS = (
    *("z0", "x0", "y0", "z1", "x1", "zk"),
    *("y1", "x2", "z2", "y2", "x3", "z3"),
    *("y3", "z4", "x4", "y4", "z5", "x5", "y5"),
)


def block_place(part, t):
    if part == "x":
        return t // 3, t + 3
    return (t + 1) // 3, jnp.where(t < 2, t + 6, t + 1)


def phase_table(points, coords, degen):
    angle = points[0][:, None] * coords[0][None, :] + points[1][:, None] * coords[1][None, :]
    angle = angle + points[2][:, None] * coords[2][None, :]
    angle = 2.0 * jnp.pi * angle
    scale = 1.0 / degen
    return (
        (jnp.cos(angle) * scale[None, :]).astype(jnp.bfloat16),
        (jnp.sin(angle) * scale[None, :]).astype(jnp.bfloat16),
    )


def ring_place(place, core, first, second):
    high = place >> 1
    low = high ^ (place & 1)
    low = low ^ jnp.where(core == 0, first, second)
    high = high ^ jnp.where(core == 0, second, first)
    return 2 * high + (low ^ high)


def widen_kernel(part, where_ref, wide_ref, narrow_ref, out_ref):
    sources = (wide_ref, narrow_ref) if part == "x" else (narrow_ref, wide_ref)
    cut = sources[0].shape[-1]
    out_ref[..., :cut] = sources[0][:, 0].astype(jnp.float32)
    out_ref[..., cut:] = sources[1][:, 0].astype(jnp.float32)


def spread(table_ref, wide_ref):
    rows = lax.broadcasted_iota(jnp.int32, (256, 32), 0)
    entry = lax.broadcasted_iota(jnp.int32, (256, 32), 1)
    pick = (rows // 8 == entry).astype(jnp.float32).astype(jnp.bfloat16)
    table = jnp.dot(pick, table_ref[...], preferred_element_type=jnp.float32).astype(jnp.bfloat16)
    table = lax.dot_general(table, pick, (((1,), (1,)), ((), ())), preferred_element_type=jnp.float32)
    rows = lax.broadcasted_iota(jnp.int32, (256, 256), 0)
    entry = lax.broadcasted_iota(jnp.int32, (256, 256), 1)
    table = jnp.where(rows % 8 == entry % 8, table, 0.0).astype(jnp.bfloat16)
    wide_ref[...] = table.reshape(8, 32, 256)


def partial_kernel(order, where_ref, wq_ref, wk_ref, even_ref, odd_ref, got_ref, *refs):
    *out_refs, mixed_ref, rows_ref, wide_ref = refs
    core, y, z, xh, xl = (where_ref[n] for n in range(5))
    lanes = got_ref.shape[-1]

    @pl.when(pl.program_id(0) == 0)
    def _():
        spread(wk_ref, wide_ref)
        for h, zf, zs in itertools.product(range(2), repeat=3):
            zat = ring_place(z, core, zf, zs)
            spot = 32 * (4 * h + 2 * zf + zs)
            rows_ref[0, spot : spot + 32] = wide_ref[(xh ^ h) * 4 + zat]
            rows_ref[1, spot : spot + 32] = wide_ref[(xh ^ h ^ core) * 4 + zat]

    for r in range(16):
        even = even_ref[r, 0].reshape(128, BLOCK)
        odd = odd_ref[r, 0].reshape(128, BLOCK)
        own = jnp.concatenate([even, odd], axis=1)
        got = got_ref[r].reshape(128, lanes).astype(jnp.bfloat16)
        rows = jnp.concatenate([own, got], axis=0)
        mixed = jnp.dot(wq_ref[...], rows, preferred_element_type=jnp.float32)
        mixed_ref[r] = mixed.reshape(2, 16, 8, lanes)
    for yf, ys, cross, other in itertools.product(range(2), repeat=4):
        g = ring_place(y, core, yf, ys) * 4 + (xl ^ cross) * 2 + (core ^ other)
        rows = mixed_ref[:, :, g].reshape(256, lanes).astype(jnp.bfloat16)
        summed = jnp.dot(rows_ref[cross], rows, preferred_element_type=jnp.float32)
        summed = summed.reshape(2, 2, 2, 2, 2, 8, lanes)
        for h, zf, zs in itertools.product(range(2), repeat=3):
            bits = {"y": (yf, ys), "z": (zf, zs), "x": (h ^ cross, h)}
            spot = sum((bits[axis] for axis in order), ())
            out_refs[spot[0]][(*spot[1:], other)] = summed[h, zf, zs]


def electron_kernel(where_ref, wk_ref, own_ref, *refs):
    *out_refs, rows_ref, wide_ref = refs
    core, z, xh = (where_ref[n] for n in (0, 2, 3))
    lanes = own_ref.shape[-1]

    @pl.when(pl.program_id(0) == 0)
    def _():
        spread(wk_ref, wide_ref)
        for zf, zs, h in itertools.product(range(2), repeat=3):
            spot = 32 * (4 * zf + 2 * zs + h)
            rows_ref[spot : spot + 32] = wide_ref[(xh ^ h) * 4 + ring_place(z, core, zf, zs)]

    for pair in range(4):
        wide = own_ref[:, 0, :, 16 * pair : 16 * pair + 16].astype(jnp.float32)
        for half in range(2):
            rows = wide[:, :, 8 * half : 8 * half + 8].reshape(256, lanes).astype(jnp.bfloat16)
            summed = jnp.dot(rows_ref[...], rows, preferred_element_type=jnp.float32)
            summed = summed.reshape(2, 2, 2, 2, 2, 8, lanes)
            for n in range(2):
                out_refs[n][:, 0, :, :, 2 * pair + half, 0] = summed[n]


def phonon_kernel(where_ref, wq_ref, own_ref, got_ref, keep_ref, send_ref, summed_ref):
    core, y, xl = (where_ref[n] for n in (0, 1, 4))
    lanes = own_ref.shape[-1]
    for h, i in itertools.product(range(2), repeat=2):
        rows = [jnp.swapaxes(ref[h, i, :, 0], 0, 1).reshape(128, lanes) for ref in (own_ref, got_ref)]
        rows = jnp.concatenate(rows, axis=0).astype(jnp.bfloat16)
        summed = jnp.dot(wq_ref[...], rows, preferred_element_type=jnp.float32)
        summed_ref[h, i] = summed.reshape(2, 16, 8, lanes)
    for xf, xs in itertools.product(range(2), repeat=2):
        h = jnp.where(core == 0, xs, xf)
        for yf, ys, other in itertools.product(range(2), repeat=3):
            g = ring_place(y, core, yf, ys) * 4 + (xl ^ xf ^ xs) * 2 + (core ^ other)
            for i in range(2):
                (keep_ref, send_ref)[xf][xs, yf, ys, other, i, 0] = summed_ref[h, i, :, g]


def kernel_call(kernel, where, inputs, in_specs, count, out, block, place, grid, scratch):
    read = sum(v.size * v.dtype.itemsize for v in inputs)
    return pl.pallas_call(
        kernel,
        grid_spec=pltpu.PrefetchScalarGridSpec(
            num_scalar_prefetch=1,
            grid=(grid,),
            in_specs=in_specs,
            out_specs=[pl.BlockSpec(block, place)] * count,
            scratch_shapes=scratch,
        ),
        out_shape=[jax.ShapeDtypeStruct(out, jnp.float32)] * count,
        compiler_params=pltpu.CompilerParams(vmem_limit_bytes=48 * 1024 * 1024),
        cost_estimate=pl.CostEstimate(
            flops=2**31, bytes_accessed=read + 4 * count * math.prod(out), transcendentals=0
        ),
    )(where, *inputs)


def electron_sums(where, wk, own):
    return kernel_call(
        electron_kernel,
        where,
        (wk, own),
        [
            pl.BlockSpec((32, 32), lambda m, w: (0, 0)),
            pl.BlockSpec((16, 1, 2, 64, FIRST), lambda m, w: (0, (2 * w[0] + m) % 4, 0, 0, 0)),
        ],
        2,
        (2, 2, 2, 2, 8, 2, 2, 8, FIRST),
        (2, 1, 2, 2, 8, 1, 2, 8, FIRST),
        lambda m, w: (0, m // 2, 0, 0, 0, m % 2, 0, 0, 0),
        4,
        [pltpu.VMEM((256, 256), jnp.bfloat16), pltpu.VMEM((8, 32, 256), jnp.bfloat16)],
    )


def phonon_sums(where, wq, own, got):
    spec = pl.BlockSpec((2, 2, 8, 1, 2, 8, FIRST), lambda u, w: (0, 0, 0, u, 0, 0, 0))
    return kernel_call(
        phonon_kernel,
        where,
        (wq, own, got),
        [pl.BlockSpec((256, 256), lambda u, w: (0, 0)), spec, spec],
        2,
        (2, 2, 2, 2, 2, 2, 2, 8, FIRST),
        (2, 2, 2, 2, 2, 1, 2, 8, FIRST),
        lambda u, w: (0, 0, 0, 0, 0, u, 0, 0, 0),
        2,
        [pltpu.VMEM((2, 2, 2, 16, 8, FIRST), jnp.float32)],
    )


def own_spec(part, block_of):
    def place(t, w):
        mode, block = block_place(part, block_of(t))
        return (0, 2 * w[0] + mode, 0, 0, block)

    return pl.BlockSpec((16, 1, 2, 64, BLOCK), place)


def widened(part, where, own):
    def spec(blocks, mode):
        lanes = blocks * BLOCK
        at = 1 if blocks == 3 else 3
        return pl.BlockSpec((4, 1, 2, 64, lanes), lambda r, w: (r, 2 * (w[0] ^ 1) + mode, 0, 0, at))

    first = 0 if part == "x" else 1
    return kernel_call(
        lambda *refs: widen_kernel(part, *refs),
        where,
        (own, own),
        [spec(3, first), spec(2, 1 - first)],
        1,
        (16, 2, 64, BLOCKS * BLOCK),
        (4, 2, 64, BLOCKS * BLOCK),
        lambda r, w: (r, 0, 0, 0),
        4,
        [],
    )[0]


def partial_sums(part, where, wq, wk, own, got):
    return kernel_call(
        lambda *refs: partial_kernel(ORDER[part], *refs),
        where,
        (wq, wk, own, own, got),
        [
            pl.BlockSpec((256, 256), lambda t, w: (0, 0)),
            pl.BlockSpec((32, 32), lambda t, w: (0, 0)),
            own_spec(part, lambda t: 2 * t),
            own_spec(part, lambda t: jnp.minimum(2 * t + 1, BLOCKS - 1)),
            pl.BlockSpec((16, 2, 64, 2 * BLOCK), lambda t, w: (0, 0, 0, t)),
        ],
        2,
        (2, 2, 2, 2, 2, 2, 2, 2, 8, BLOCKS * BLOCK),
        (2, 2, 2, 2, 2, 2, 2, 2, 8, 2 * BLOCK),
        lambda t, w: (0, 0, 0, 0, 0, 0, 0, 0, 0, t),
        PAIRS,
        [
            pltpu.VMEM((16, 2, 16, 8, 2 * BLOCK), jnp.float32),
            pltpu.VMEM((2, 256, 256), jnp.bfloat16),
            pltpu.VMEM((8, 32, 256), jnp.bfloat16),
        ],
    )


def exchange(value, axis, step):
    pairs = []
    for core in range(2):
        for at in range(4):
            to = at ^ 1 if core == step else 3 - at
            if axis == "z":
                pairs.append((core * 4 + at, core * 4 + to))
            elif axis == "y":
                pairs.append((at * 2 + core, to * 2 + core))
            else:
                pairs.append(((at % 2) * 4 + core * 2 + at // 2, (to % 2) * 4 + core * 2 + to // 2))
    names = {"z": ("c", "z"), "y": ("y", "c"), "x": ("xl", "c", "xh")}[axis]
    return lax.ppermute(value, names, pairs)


def swap(value):
    return lax.ppermute(value, "c", [(0, 1), (1, 0)])


def rotation_tables(rot_right, rot_left):
    r_real, r_imag = (rot_right[:, 0], rot_right[:, 1])
    l_real, l_imag = (rot_left[:, :, 0], rot_left[:, :, 1])
    right = jnp.stack([jnp.stack([r_real, r_imag], 2), jnp.stack([-r_imag, r_real], 2)], 1)
    left = jnp.stack([jnp.stack([l_real, -l_imag], 3), jnp.stack([l_imag, l_real], 3)], 2)
    right = right.transpose(0, 1, 3, 2, 4)[:, :, :, None, :, None, :]
    right = right * jnp.eye(8, dtype=jnp.float32)[:, None, :, None]
    left = left.transpose(0, 1, 4, 5, 2, 3)
    return right.reshape(2, 2, 2, 256, 256), left.reshape(2, 8, 64, 64)


def split(value):
    high = value.astype(jnp.bfloat16)
    return high, (value - high.astype(jnp.float32)).astype(jnp.bfloat16)


def dot(left, right):
    return jnp.dot(left, right, preferred_element_type=jnp.float32)


def regroup(parts):
    group = lax.broadcasted_iota(jnp.int32, (8, 128), 1) // 32
    out = []
    for n in range(4):
        total = parts[n]
        for m in range(4):
            if m != n:
                total = jnp.where(group == m, pltpu.roll(parts[m], 32 * (m - n) % 128, 1), total)
        out.append(total)
    return out


def rotation_kernel(sum_ref, right_ref, left_ref, out_ref, turned_ref, done_ref):
    turned = [0.0, 0.0]
    for p in range(2):
        rows = sum_ref[0, p].reshape(32, 1024)
        rows = jnp.concatenate([rows[:, 256 * t : 256 * t + 256] for t in range(4)], axis=0)
        high, low = split(rows)
        both = jnp.concatenate([high, low], axis=0)
        for s in range(2):
            right_high, right_low = split(right_ref[0, p, s])
            product = dot(both, right_high)
            turned[s] = turned[s] + product[:128] + product[128:] + dot(high, right_low)
    for s in range(2):
        blocks = turned[s].reshape(4, 4, 8, 256)
        for t in range(8):
            parts = [blocks[t // 2, m, :, 128 * (t % 2) : 128 * (t % 2) + 128] for m in range(4)]
            for n, part in enumerate(regroup(parts)):
                spot = 8 * (32 * s + 4 * t + n)
                turned_ref[spot : spot + 8] = part
    for j in range(8):
        high, low = split(turned_ref[pl.ds(j, 64, stride=8), :])
        left_high, left_low = split(left_ref[0, j])
        product = dot(jnp.concatenate([left_high, left_low], axis=0), high)
        done_ref[pl.ds(j, 64, stride=8), :] = product[:64] + product[64:] + dot(left_high, low)
    for s in range(2):
        for t in range(8):
            spot = 8 * (32 * s + 4 * t)
            parts = [done_ref[spot + 8 * n : spot + 8 * n + 8] for n in range(4)]
            for m, part in enumerate(regroup(parts)):
                out_ref[0, :, m, s, 128 * t : 128 * t + 128] = part


def rotate(summed, right, left):
    return pl.pallas_call(
        rotation_kernel,
        grid=(2,),
        in_specs=[
            pl.BlockSpec((1, 2, 4, 8, 1024), lambda k: (k, 0, 0, 0, 0)),
            pl.BlockSpec((1, 2, 2, 256, 256), lambda k: (k, 0, 0, 0, 0)),
            pl.BlockSpec((1, 8, 64, 64), lambda k: (k, 0, 0, 0)),
        ],
        out_specs=pl.BlockSpec((1, 8, 4, 2, 1024), lambda k: (k, 0, 0, 0, 0)),
        out_shape=jax.ShapeDtypeStruct((2, 8, 4, 2, 1024), jnp.float32),
        scratch_shapes=[pltpu.VMEM((512, 128), jnp.float32)] * 2,
        compiler_params=pltpu.CompilerParams(vmem_limit_bytes=48 * 1024 * 1024),
        cost_estimate=pl.CostEstimate(flops=2**28, bytes_accessed=2**22, transcendentals=0),
    )(summed, right, left)


def complex_table(cos_part, sin_part):
    top = jnp.concatenate([cos_part, -sin_part], axis=1)
    bottom = jnp.concatenate([sin_part, cos_part], axis=1)
    return jnp.concatenate([top, bottom], axis=0)


def body(
    wannier_g, el_vectors, ph_vectors, el_degen, ph_degen, k_points, q_points, rot_right, rot_left
):
    core = lax.axis_index("c")
    where = jnp.stack([core, *(lax.axis_index(a) for a in ("y", "z", "xh", "xl"))]).astype(jnp.int32)

    vectors = jnp.concatenate([ph_vectors, ph_degen[None]], axis=0).astype(jnp.float32)
    others = swap(vectors)
    k_cos, k_sin = phase_table(k_points, el_vectors.astype(jnp.float32), el_degen.astype(jnp.float32))
    wide = jnp.stack([jnp.stack([k_cos, -k_sin], 2), jnp.stack([k_sin, k_cos], 2)], 1)
    wk = wide.reshape(32, 32)
    tables = [complex_table(*phase_table(q_points, v[:3], v[3])) for v in (vectors, others)]
    wq = jnp.concatenate(tables, axis=1)

    own = lax.optimization_barrier(wannier_g.transpose(0, 2, 3, 1, 4))

    def after(earlier, *values):
        return lax.optimization_barrier((*values, earlier))[:-1]

    keep, send, arrived = {}, {}, {}

    def begin(part, sums):
        keep[part], send[part] = sums
        arrived[part] = exchange(send[part], part, 0)

    (own,) = after(others, own)
    got_x = widened("x", where, own)
    (later,) = after(got_x, own)
    got_x = swap(got_x)
    got_y = widened("y", where, later)
    (wk,) = after(got_y, wk)
    got_y = swap(got_y)
    begin("z", electron_sums(where, wk, own))
    wq, got_x = after(keep["z"], wq, got_x)
    begin("x", partial_sums("x", where, wq, wk, own, got_x))
    wq, got_y = after(keep["x"], wq, got_y)
    begin("y", partial_sums("y", where, wq, wk, own, got_y))
    rot_right, rot_left = after(keep["y"], rot_right, rot_left)
    right, left = rotation_tables(rot_right, rot_left)
    latest = (right, left, keep["y"])
    for event in EVENTS:
        part, step = event
        axes = ORDER[part]
        (arrived[part],) = after(latest, arrived[part])
        if step == "0":
            latest = send[part] = keep[part][1] + arrived[part][1]
            held, came = after(latest, keep[part], arrived[part])
            arrived[part] = exchange(send[part], axes[0], 1)
            keep[part] = held[0] + came[0]
        elif step == "k":
            keep[part], send[part] = phonon_sums(where, wq, keep[part], arrived[part])
            arrived[part] = exchange(send[part], axes[1], 0)
            latest = keep[part]
        elif step == "5":
            latest = keep[part] = keep[part] + arrived[part]
        else:
            latest = send[part] = keep[part][1] + arrived[part][1]
            keep[part] = keep[part][0] + arrived[part][0]
            if event == "z1":
                arrived[part] = swap(send[part])
            else:
                arrived[part] = exchange(send[part], axes[(int(step) + 1) // 2], (int(step) + 1) % 2)

    modes = []
    for ours in (True, False):
        z, x, y = (keep[part][0] if ours else swap(keep[part][1]) for part in "zxy")
        wide, narrow = 3 * BLOCK, 2 * BLOCK
        modes.append(jnp.concatenate([z[:, 0], x[..., :wide], y[..., :narrow]], axis=-1))
        modes.append(jnp.concatenate([z[:, 1], y[..., narrow:], x[..., wide:]], axis=-1))
    mine, theirs = jnp.stack(modes[:2], axis=2), jnp.stack(modes[2:], axis=2)
    modes = jnp.concatenate([jnp.where(core == 0, mine, theirs), jnp.where(core == 0, theirs, mine)], axis=2)
    return rotate(modes, right, left)


def solution(mesh):
    fine = Mesh(mesh.devices.reshape(4, 2, 2, 2, 4), ("y", "xl", "c", "xh", "z"))
    ph, el = ("y", "xl", "c"), ("xh", "z")
    in_specs = (
        P(el, ph, None, None, None),
        P(None, el),
        P(None, ph),
        P(el),
        P(ph),
        P(),
        P(),
        P(el, None, None, None),
        P(el, ph, None, None, None),
    )
    out_specs = P(el, ph, None, None, None)
    return jax.shard_map(body, mesh=fine, in_specs=in_specs, out_specs=out_specs, check_vma=False)
```

```python
import itertools
import math

import jax
import jax.numpy as jnp
from jax import lax
from jax.experimental import pallas as pl
from jax.experimental.pallas import tpu as pltpu
from jax.sharding import Mesh, PartitionSpec as P

FIRST = 384
BLOCK = 128
BLOCKS = 5
PAIRS = 3
ORDER = {"z": "zxy", "x": "xyz", "y": "yzx"}
EVENTS = (
    *("z0", "x0", "y0", "z1", "x1", "zk"),
    *("y1", "x2", "z2", "y2", "x3", "z3"),
    *("y3", "z4", "x4", "y4", "z5", "x5", "y5"),
)


def block_place(part, t):
    if part == "x":
        return t // 3, t + 3
    return (t + 1) // 3, jnp.where(t < 2, t + 6, t + 1)


def phase_table(points, coords, degen):
    angle = points[0][:, None] * coords[0][None, :] + points[1][:, None] * coords[1][None, :]
    angle = angle + points[2][:, None] * coords[2][None, :]
    angle = 2.0 * jnp.pi * angle
    scale = 1.0 / degen
    return (
        (jnp.cos(angle) * scale[None, :]).astype(jnp.bfloat16),
        (jnp.sin(angle) * scale[None, :]).astype(jnp.bfloat16),
    )


def ring_place(place, core, first, second):
    high = place >> 1
    low = high ^ (place & 1)
    low = low ^ jnp.where(core == 0, first, second)
    high = high ^ jnp.where(core == 0, second, first)
    return 2 * high + (low ^ high)


def widen_kernel(part, where_ref, wide_ref, narrow_ref, out_ref):
    sources = (wide_ref, narrow_ref) if part == "x" else (narrow_ref, wide_ref)
    cut = sources[0].shape[-1]
    out_ref[..., :cut] = sources[0][:, 0].astype(jnp.float32)
    out_ref[..., cut:] = sources[1][:, 0].astype(jnp.float32)


def spread(table_ref, wide_ref):
    rows = lax.broadcasted_iota(jnp.int32, (256, 32), 0)
    entry = lax.broadcasted_iota(jnp.int32, (256, 32), 1)
    pick = (rows // 8 == entry).astype(jnp.float32).astype(jnp.bfloat16)
    table = jnp.dot(pick, table_ref[...], preferred_element_type=jnp.float32).astype(jnp.bfloat16)
    table = lax.dot_general(table, pick, (((1,), (1,)), ((), ())), preferred_element_type=jnp.float32)
    rows = lax.broadcasted_iota(jnp.int32, (256, 256), 0)
    entry = lax.broadcasted_iota(jnp.int32, (256, 256), 1)
    table = jnp.where(rows % 8 == entry % 8, table, 0.0).astype(jnp.bfloat16)
    wide_ref[...] = table.reshape(8, 32, 256)


def partial_kernel(order, where_ref, wq_ref, wk_ref, even_ref, odd_ref, got_ref, *refs):
    *out_refs, mixed_ref, rows_ref, wide_ref = refs
    core, y, z, xh, xl = (where_ref[n] for n in range(5))
    lanes = got_ref.shape[-1]

    @pl.when(pl.program_id(0) == 0)
    def _():
        spread(wk_ref, wide_ref)
        for h, zf, zs in itertools.product(range(2), repeat=3):
            zat = ring_place(z, core, zf, zs)
            spot = 32 * (4 * h + 2 * zf + zs)
            rows_ref[0, spot : spot + 32] = wide_ref[(xh ^ h) * 4 + zat]
            rows_ref[1, spot : spot + 32] = wide_ref[(xh ^ h ^ core) * 4 + zat]

    for r in range(16):
        even = even_ref[r, 0].reshape(128, BLOCK)
        odd = odd_ref[r, 0].reshape(128, BLOCK)
        own = jnp.concatenate([even, odd], axis=1)
        got = got_ref[r].reshape(128, lanes).astype(jnp.bfloat16)
        rows = jnp.concatenate([own, got], axis=0)
        mixed = jnp.dot(wq_ref[...], rows, preferred_element_type=jnp.float32)
        mixed_ref[r] = mixed.reshape(2, 16, 8, lanes)
    for yf, ys, cross, other in itertools.product(range(2), repeat=4):
        g = ring_place(y, core, yf, ys) * 4 + (xl ^ cross) * 2 + (core ^ other)
        rows = mixed_ref[:, :, g].reshape(256, lanes).astype(jnp.bfloat16)
        summed = jnp.dot(rows_ref[cross], rows, preferred_element_type=jnp.float32)
        summed = summed.reshape(2, 2, 2, 2, 2, 8, lanes)
        for h, zf, zs in itertools.product(range(2), repeat=3):
            bits = {"y": (yf, ys), "z": (zf, zs), "x": (h ^ cross, h)}
            spot = sum((bits[axis] for axis in order), ())
            out_refs[spot[0]][(*spot[1:], other)] = summed[h, zf, zs]


def electron_kernel(where_ref, wk_ref, own_ref, *refs):
    *out_refs, rows_ref, wide_ref = refs
    core, z, xh = (where_ref[n] for n in (0, 2, 3))
    lanes = own_ref.shape[-1]

    @pl.when(pl.program_id(0) == 0)
    def _():
        spread(wk_ref, wide_ref)
        for zf, zs, h in itertools.product(range(2), repeat=3):
            spot = 32 * (4 * zf + 2 * zs + h)
            rows_ref[spot : spot + 32] = wide_ref[(xh ^ h) * 4 + ring_place(z, core, zf, zs)]

    for pair in range(4):
        wide = own_ref[:, 0, :, 16 * pair : 16 * pair + 16].astype(jnp.float32)
        for half in range(2):
            rows = wide[:, :, 8 * half : 8 * half + 8].reshape(256, lanes).astype(jnp.bfloat16)
            summed = jnp.dot(rows_ref[...], rows, preferred_element_type=jnp.float32)
            summed = summed.reshape(2, 2, 2, 2, 2, 8, lanes)
            for n in range(2):
                out_refs[n][:, 0, :, :, 2 * pair + half, 0] = summed[n]


def phonon_kernel(where_ref, wq_ref, own_ref, got_ref, keep_ref, send_ref, summed_ref):
    core, y, xl = (where_ref[n] for n in (0, 1, 4))
    lanes = own_ref.shape[-1]
    for h, i in itertools.product(range(2), repeat=2):
        rows = [jnp.swapaxes(ref[h, i, :, 0], 0, 1).reshape(128, lanes) for ref in (own_ref, got_ref)]
        rows = jnp.concatenate(rows, axis=0).astype(jnp.bfloat16)
        summed = jnp.dot(wq_ref[...], rows, preferred_element_type=jnp.float32)
        summed_ref[h, i] = summed.reshape(2, 16, 8, lanes)
    for xf, xs in itertools.product(range(2), repeat=2):
        h = jnp.where(core == 0, xs, xf)
        for yf, ys, other in itertools.product(range(2), repeat=3):
            g = ring_place(y, core, yf, ys) * 4 + (xl ^ xf ^ xs) * 2 + (core ^ other)
            for i in range(2):
                (keep_ref, send_ref)[xf][xs, yf, ys, other, i, 0] = summed_ref[h, i, :, g]


def kernel_call(kernel, where, inputs, in_specs, count, out, block, place, grid, scratch):
    read = sum(v.size * v.dtype.itemsize for v in inputs)
    return pl.pallas_call(
        kernel,
        grid_spec=pltpu.PrefetchScalarGridSpec(
            num_scalar_prefetch=1,
            grid=(grid,),
            in_specs=in_specs,
            out_specs=[pl.BlockSpec(block, place)] * count,
            scratch_shapes=scratch,
        ),
        out_shape=[jax.ShapeDtypeStruct(out, jnp.float32)] * count,
        compiler_params=pltpu.CompilerParams(vmem_limit_bytes=48 * 1024 * 1024),
        cost_estimate=pl.CostEstimate(
            flops=2**31, bytes_accessed=read + 4 * count * math.prod(out), transcendentals=0
        ),
    )(where, *inputs)


def electron_sums(where, wk, own):
    return kernel_call(
        electron_kernel,
        where,
        (wk, own),
        [
            pl.BlockSpec((32, 32), lambda m, w: (0, 0)),
            pl.BlockSpec((16, 1, 2, 64, FIRST), lambda m, w: (0, (2 * w[0] + m) % 4, 0, 0, 0)),
        ],
        2,
        (2, 2, 2, 2, 8, 2, 2, 8, FIRST),
        (2, 1, 2, 2, 8, 1, 2, 8, FIRST),
        lambda m, w: (0, m // 2, 0, 0, 0, m % 2, 0, 0, 0),
        4,
        [pltpu.VMEM((256, 256), jnp.bfloat16), pltpu.VMEM((8, 32, 256), jnp.bfloat16)],
    )


def phonon_sums(where, wq, own, got):
    spec = pl.BlockSpec((2, 2, 8, 1, 2, 8, FIRST), lambda u, w: (0, 0, 0, u, 0, 0, 0))
    return kernel_call(
        phonon_kernel,
        where,
        (wq, own, got),
        [pl.BlockSpec((256, 256), lambda u, w: (0, 0)), spec, spec],
        2,
        (2, 2, 2, 2, 2, 2, 2, 8, FIRST),
        (2, 2, 2, 2, 2, 1, 2, 8, FIRST),
        lambda u, w: (0, 0, 0, 0, 0, u, 0, 0, 0),
        2,
        [pltpu.VMEM((2, 2, 2, 16, 8, FIRST), jnp.float32)],
    )


def own_spec(part, block_of):
    def place(t, w):
        mode, block = block_place(part, block_of(t))
        return (0, 2 * w[0] + mode, 0, 0, block)

    return pl.BlockSpec((16, 1, 2, 64, BLOCK), place)


def widened(part, where, own):
    def spec(blocks, mode):
        lanes = blocks * BLOCK
        at = 1 if blocks == 3 else 3
        return pl.BlockSpec((8, 1, 2, 64, lanes), lambda r, w: (r, 2 * (w[0] ^ 1) + mode, 0, 0, at))

    first = 0 if part == "x" else 1
    return kernel_call(
        lambda *refs: widen_kernel(part, *refs),
        where,
        (own, own),
        [spec(3, first), spec(2, 1 - first)],
        1,
        (16, 2, 64, BLOCKS * BLOCK),
        (8, 2, 64, BLOCKS * BLOCK),
        lambda r, w: (r, 0, 0, 0),
        2,
        [],
    )[0]


def partial_sums(part, where, wq, wk, own, got):
    return kernel_call(
        lambda *refs: partial_kernel(ORDER[part], *refs),
        where,
        (wq, wk, own, own, got),
        [
            pl.BlockSpec((256, 256), lambda t, w: (0, 0)),
            pl.BlockSpec((32, 32), lambda t, w: (0, 0)),
            own_spec(part, lambda t: 2 * t),
            own_spec(part, lambda t: jnp.minimum(2 * t + 1, BLOCKS - 1)),
            pl.BlockSpec((16, 2, 64, 2 * BLOCK), lambda t, w: (0, 0, 0, t)),
        ],
        2,
        (2, 2, 2, 2, 2, 2, 2, 2, 8, BLOCKS * BLOCK),
        (2, 2, 2, 2, 2, 2, 2, 2, 8, 2 * BLOCK),
        lambda t, w: (0, 0, 0, 0, 0, 0, 0, 0, 0, t),
        PAIRS,
        [
            pltpu.VMEM((16, 2, 16, 8, 2 * BLOCK), jnp.float32),
            pltpu.VMEM((2, 256, 256), jnp.bfloat16),
            pltpu.VMEM((8, 32, 256), jnp.bfloat16),
        ],
    )


def exchange(value, axis, step):
    pairs = []
    for core in range(2):
        for at in range(4):
            to = at ^ 1 if core == step else 3 - at
            if axis == "z":
                pairs.append((core * 4 + at, core * 4 + to))
            elif axis == "y":
                pairs.append((at * 2 + core, to * 2 + core))
            else:
                pairs.append(((at % 2) * 4 + core * 2 + at // 2, (to % 2) * 4 + core * 2 + to // 2))
    names = {"z": ("c", "z"), "y": ("y", "c"), "x": ("xl", "c", "xh")}[axis]
    return lax.ppermute(value, names, pairs)


def swap(value):
    return lax.ppermute(value, "c", [(0, 1), (1, 0)])


def rotation_tables(rot_right, rot_left):
    r_real, r_imag = (rot_right[:, 0], rot_right[:, 1])
    l_real, l_imag = (rot_left[:, :, 0], rot_left[:, :, 1])
    right = jnp.stack([jnp.stack([r_real, r_imag], 2), jnp.stack([-r_imag, r_real], 2)], 1)
    left = jnp.stack([jnp.stack([l_real, -l_imag], 3), jnp.stack([l_imag, l_real], 3)], 2)
    right = right.transpose(0, 1, 3, 2, 4)[:, :, :, None, :, None, :]
    right = right * jnp.eye(8, dtype=jnp.float32)[:, None, :, None]
    left = left.transpose(0, 1, 4, 5, 2, 3)
    return right.reshape(2, 2, 2, 256, 256), left.reshape(2, 8, 64, 64)


def split(value):
    high = value.astype(jnp.bfloat16)
    return high, (value - high.astype(jnp.float32)).astype(jnp.bfloat16)


def dot(left, right):
    return jnp.dot(left, right, preferred_element_type=jnp.float32)


def regroup(parts):
    group = lax.broadcasted_iota(jnp.int32, (8, 128), 1) // 32
    out = []
    for n in range(4):
        total = parts[n]
        for m in range(4):
            if m != n:
                total = jnp.where(group == m, pltpu.roll(parts[m], 32 * (m - n) % 128, 1), total)
        out.append(total)
    return out


def rotation_kernel(sum_ref, right_ref, left_ref, out_ref, turned_ref, done_ref):
    turned = [0.0, 0.0]
    for p in range(2):
        rows = sum_ref[0, p].reshape(32, 1024)
        rows = jnp.concatenate([rows[:, 256 * t : 256 * t + 256] for t in range(4)], axis=0)
        high, low = split(rows)
        both = jnp.concatenate([high, low], axis=0)
        for s in range(2):
            right_high, right_low = split(right_ref[0, p, s])
            product = dot(both, right_high)
            turned[s] = turned[s] + product[:128] + product[128:] + dot(high, right_low)
    for s in range(2):
        blocks = turned[s].reshape(4, 4, 8, 256)
        for t in range(8):
            parts = [blocks[t // 2, m, :, 128 * (t % 2) : 128 * (t % 2) + 128] for m in range(4)]
            for n, part in enumerate(regroup(parts)):
                spot = 8 * (32 * s + 4 * t + n)
                turned_ref[spot : spot + 8] = part
    for j in range(8):
        high, low = split(turned_ref[pl.ds(j, 64, stride=8), :])
        left_high, left_low = split(left_ref[0, j])
        product = dot(jnp.concatenate([left_high, left_low], axis=0), high)
        done_ref[pl.ds(j, 64, stride=8), :] = product[:64] + product[64:] + dot(left_high, low)
    for s in range(2):
        for t in range(8):
            spot = 8 * (32 * s + 4 * t)
            parts = [done_ref[spot + 8 * n : spot + 8 * n + 8] for n in range(4)]
            for m, part in enumerate(regroup(parts)):
                out_ref[0, :, m, s, 128 * t : 128 * t + 128] = part


def rotate(summed, right, left):
    return pl.pallas_call(
        rotation_kernel,
        grid=(2,),
        in_specs=[
            pl.BlockSpec((1, 2, 4, 8, 1024), lambda k: (k, 0, 0, 0, 0)),
            pl.BlockSpec((1, 2, 2, 256, 256), lambda k: (k, 0, 0, 0, 0)),
            pl.BlockSpec((1, 8, 64, 64), lambda k: (k, 0, 0, 0)),
        ],
        out_specs=pl.BlockSpec((1, 8, 4, 2, 1024), lambda k: (k, 0, 0, 0, 0)),
        out_shape=jax.ShapeDtypeStruct((2, 8, 4, 2, 1024), jnp.float32),
        scratch_shapes=[pltpu.VMEM((512, 128), jnp.float32)] * 2,
        compiler_params=pltpu.CompilerParams(vmem_limit_bytes=48 * 1024 * 1024),
        cost_estimate=pl.CostEstimate(flops=2**28, bytes_accessed=2**22, transcendentals=0),
    )(summed, right, left)


def complex_table(cos_part, sin_part):
    top = jnp.concatenate([cos_part, -sin_part], axis=1)
    bottom = jnp.concatenate([sin_part, cos_part], axis=1)
    return jnp.concatenate([top, bottom], axis=0)


def body(
    wannier_g, el_vectors, ph_vectors, el_degen, ph_degen, k_points, q_points, rot_right, rot_left
):
    core = lax.axis_index("c")
    where = jnp.stack([core, *(lax.axis_index(a) for a in ("y", "z", "xh", "xl"))]).astype(jnp.int32)

    vectors = jnp.concatenate([ph_vectors, ph_degen[None]], axis=0).astype(jnp.float32)
    others = swap(vectors)
    k_cos, k_sin = phase_table(k_points, el_vectors.astype(jnp.float32), el_degen.astype(jnp.float32))
    wide = jnp.stack([jnp.stack([k_cos, -k_sin], 2), jnp.stack([k_sin, k_cos], 2)], 1)
    wk = wide.reshape(32, 32)
    tables = [complex_table(*phase_table(q_points, v[:3], v[3])) for v in (vectors, others)]
    wq = jnp.concatenate(tables, axis=1)

    own = lax.optimization_barrier(wannier_g.transpose(0, 2, 3, 1, 4))

    def after(earlier, *values):
        return lax.optimization_barrier((*values, earlier))[:-1]

    keep, send, arrived = {}, {}, {}

    def begin(part, sums):
        keep[part], send[part] = sums
        arrived[part] = exchange(send[part], part, 0)

    (own,) = after(others, own)
    got_x = widened("x", where, own)
    (later,) = after(got_x, own)
    got_x = swap(got_x)
    got_y = widened("y", where, later)
    (wk,) = after(got_y, wk)
    got_y = swap(got_y)
    begin("z", electron_sums(where, wk, own))
    wq, got_x = after(keep["z"], wq, got_x)
    begin("x", partial_sums("x", where, wq, wk, own, got_x))
    wq, got_y = after(keep["x"], wq, got_y)
    begin("y", partial_sums("y", where, wq, wk, own, got_y))
    rot_right, rot_left = after(keep["y"], rot_right, rot_left)
    right, left = rotation_tables(rot_right, rot_left)
    latest = (right, left, keep["y"])
    for event in EVENTS:
        part, step = event
        axes = ORDER[part]
        (arrived[part],) = after(latest, arrived[part])
        if step == "0":
            latest = send[part] = keep[part][1] + arrived[part][1]
            held, came = after(latest, keep[part], arrived[part])
            arrived[part] = exchange(send[part], axes[0], 1)
            keep[part] = held[0] + came[0]
        elif step == "k":
            keep[part], send[part] = phonon_sums(where, wq, keep[part], arrived[part])
            arrived[part] = exchange(send[part], axes[1], 0)
            latest = keep[part]
        elif step == "5":
            latest = keep[part] = keep[part] + arrived[part]
        else:
            latest = send[part] = keep[part][1] + arrived[part][1]
            keep[part] = keep[part][0] + arrived[part][0]
            if event == "z1":
                arrived[part] = swap(send[part])
            else:
                arrived[part] = exchange(send[part], axes[(int(step) + 1) // 2], (int(step) + 1) % 2)

    modes = []
    for ours in (True, False):
        z, x, y = (keep[part][0] if ours else swap(keep[part][1]) for part in "zxy")
        wide, narrow = 3 * BLOCK, 2 * BLOCK
        modes.append(jnp.concatenate([z[:, 0], x[..., :wide], y[..., :narrow]], axis=-1))
        modes.append(jnp.concatenate([z[:, 1], y[..., narrow:], x[..., wide:]], axis=-1))
    mine, theirs = jnp.stack(modes[:2], axis=2), jnp.stack(modes[2:], axis=2)
    modes = jnp.concatenate([jnp.where(core == 0, mine, theirs), jnp.where(core == 0, theirs, mine)], axis=2)
    return rotate(modes, right, left)


def solution(mesh):
    fine = Mesh(mesh.devices.reshape(4, 2, 2, 2, 4), ("y", "xl", "c", "xh", "z"))
    ph, el = ("y", "xl", "c"), ("xh", "z")
    in_specs = (
        P(el, ph, None, None, None),
        P(None, el),
        P(None, ph),
        P(el),
        P(ph),
        P(),
        P(),
        P(el, None, None, None),
        P(el, ph, None, None, None),
    )
    out_specs = P(el, ph, None, None, None)
    return jax.shard_map(body, mesh=fine, in_specs=in_specs, out_specs=out_specs, check_vma=False)
```

```python
import itertools
import math

import jax
import jax.numpy as jnp
from jax import lax
from jax.experimental import pallas as pl
from jax.experimental.pallas import tpu as pltpu
from jax.sharding import Mesh, PartitionSpec as P

FIRST = 384
BLOCK = 128
BLOCKS = 5
PAIRS = 3
ORDER = {"z": "zxy", "x": "xyz", "y": "yzx"}
EVENTS = (
    *("z0", "x0", "y0", "z1", "x1", "zk"),
    *("y1", "x2", "z2", "y2", "x3", "z3"),
    *("y3", "z4", "x4", "y4", "z5", "x5", "y5"),
)


def block_place(part, t):
    if part == "x":
        return t // 3, t + 3
    return (t + 1) // 3, jnp.where(t < 2, t + 6, t + 1)


def phase_table(points, coords, degen):
    angle = points[0][:, None] * coords[0][None, :] + points[1][:, None] * coords[1][None, :]
    angle = angle + points[2][:, None] * coords[2][None, :]
    angle = 2.0 * jnp.pi * angle
    scale = 1.0 / degen
    return (
        (jnp.cos(angle) * scale[None, :]).astype(jnp.bfloat16),
        (jnp.sin(angle) * scale[None, :]).astype(jnp.bfloat16),
    )


def ring_place(place, core, first, second):
    high = place >> 1
    low = high ^ (place & 1)
    low = low ^ jnp.where(core == 0, first, second)
    high = high ^ jnp.where(core == 0, second, first)
    return 2 * high + (low ^ high)


def widen_kernel(part, where_ref, wide_ref, narrow_ref, out_ref):
    sources = (wide_ref, narrow_ref) if part == "x" else (narrow_ref, wide_ref)
    cut = sources[0].shape[-1]
    out_ref[..., :cut] = sources[0][:, 0].astype(jnp.float32)
    out_ref[..., cut:] = sources[1][:, 0].astype(jnp.float32)


def spread(table_ref, wide_ref):
    rows = lax.broadcasted_iota(jnp.int32, (256, 32), 0)
    entry = lax.broadcasted_iota(jnp.int32, (256, 32), 1)
    pick = (rows // 8 == entry).astype(jnp.float32).astype(jnp.bfloat16)
    table = jnp.dot(pick, table_ref[...], preferred_element_type=jnp.float32).astype(jnp.bfloat16)
    table = lax.dot_general(table, pick, (((1,), (1,)), ((), ())), preferred_element_type=jnp.float32)
    rows = lax.broadcasted_iota(jnp.int32, (256, 256), 0)
    entry = lax.broadcasted_iota(jnp.int32, (256, 256), 1)
    table = jnp.where(rows % 8 == entry % 8, table, 0.0).astype(jnp.bfloat16)
    wide_ref[...] = table.reshape(8, 32, 256)


def partial_kernel(order, where_ref, wq_ref, wk_ref, even_ref, odd_ref, got_ref, *refs):
    *out_refs, mixed_ref, rows_ref, wide_ref = refs
    core, y, z, xh, xl = (where_ref[n] for n in range(5))
    lanes = got_ref.shape[-1]

    @pl.when(pl.program_id(0) == 0)
    def _():
        spread(wk_ref, wide_ref)
        for h, zf, zs in itertools.product(range(2), repeat=3):
            zat = ring_place(z, core, zf, zs)
            spot = 32 * (4 * h + 2 * zf + zs)
            rows_ref[0, spot : spot + 32] = wide_ref[(xh ^ h) * 4 + zat]
            rows_ref[1, spot : spot + 32] = wide_ref[(xh ^ h ^ core) * 4 + zat]

    for r in range(16):
        even = even_ref[r, 0].reshape(128, BLOCK)
        odd = odd_ref[r, 0].reshape(128, BLOCK)
        own = jnp.concatenate([even, odd], axis=1)
        got = got_ref[r].reshape(128, lanes).astype(jnp.bfloat16)
        rows = jnp.concatenate([own, got], axis=0)
        mixed = jnp.dot(wq_ref[...], rows, preferred_element_type=jnp.float32)
        mixed_ref[r] = mixed.reshape(2, 16, 8, lanes)
    for yf, ys, cross, other in itertools.product(range(2), repeat=4):
        g = ring_place(y, core, yf, ys) * 4 + (xl ^ cross) * 2 + (core ^ other)
        rows = mixed_ref[:, :, g].reshape(256, lanes).astype(jnp.bfloat16)
        summed = jnp.dot(rows_ref[cross], rows, preferred_element_type=jnp.float32)
        summed = summed.reshape(2, 2, 2, 2, 2, 8, lanes)
        for h, zf, zs in itertools.product(range(2), repeat=3):
            bits = {"y": (yf, ys), "z": (zf, zs), "x": (h ^ cross, h)}
            spot = sum((bits[axis] for axis in order), ())
            out_refs[spot[0]][(*spot[1:], other)] = summed[h, zf, zs]


def electron_kernel(where_ref, wk_ref, own_ref, *refs):
    *out_refs, rows_ref, wide_ref = refs
    core, z, xh = (where_ref[n] for n in (0, 2, 3))
    lanes = own_ref.shape[-1]

    @pl.when(pl.program_id(0) == 0)
    def _():
        spread(wk_ref, wide_ref)
        for zf, zs, h in itertools.product(range(2), repeat=3):
            spot = 32 * (4 * zf + 2 * zs + h)
            rows_ref[spot : spot + 32] = wide_ref[(xh ^ h) * 4 + ring_place(z, core, zf, zs)]

    for pair in range(4):
        wide = own_ref[:, 0, :, 16 * pair : 16 * pair + 16].astype(jnp.float32)
        for half in range(2):
            rows = wide[:, :, 8 * half : 8 * half + 8].reshape(256, lanes).astype(jnp.bfloat16)
            summed = jnp.dot(rows_ref[...], rows, preferred_element_type=jnp.float32)
            summed = summed.reshape(2, 2, 2, 2, 2, 8, lanes)
            for n in range(2):
                out_refs[n][:, 0, :, :, 2 * pair + half, 0] = summed[n]


def phonon_kernel(where_ref, wq_ref, own_ref, got_ref, keep_ref, send_ref, summed_ref):
    core, y, xl = (where_ref[n] for n in (0, 1, 4))
    lanes = own_ref.shape[-1]
    for h, i in itertools.product(range(2), repeat=2):
        rows = [jnp.swapaxes(ref[h, i, :, 0], 0, 1).reshape(128, lanes) for ref in (own_ref, got_ref)]
        rows = jnp.concatenate(rows, axis=0).astype(jnp.bfloat16)
        summed = jnp.dot(wq_ref[...], rows, preferred_element_type=jnp.float32)
        summed_ref[h, i] = summed.reshape(2, 16, 8, lanes)
    for xf, xs in itertools.product(range(2), repeat=2):
        h = jnp.where(core == 0, xs, xf)
        for yf, ys, other in itertools.product(range(2), repeat=3):
            g = ring_place(y, core, yf, ys) * 4 + (xl ^ xf ^ xs) * 2 + (core ^ other)
            for i in range(2):
                (keep_ref, send_ref)[xf][xs, yf, ys, other, i, 0] = summed_ref[h, i, :, g]


def kernel_call(kernel, where, inputs, in_specs, count, out, block, place, grid, scratch, vmem=48):
    read = sum(v.size * v.dtype.itemsize for v in inputs)
    return pl.pallas_call(
        kernel,
        grid_spec=pltpu.PrefetchScalarGridSpec(
            num_scalar_prefetch=1,
            grid=(grid,),
            in_specs=in_specs,
            out_specs=[pl.BlockSpec(block, place)] * count,
            scratch_shapes=scratch,
        ),
        out_shape=[jax.ShapeDtypeStruct(out, jnp.float32)] * count,
        compiler_params=pltpu.CompilerParams(vmem_limit_bytes=vmem * 1024 * 1024),
        cost_estimate=pl.CostEstimate(
            flops=2**31, bytes_accessed=read + 4 * count * math.prod(out), transcendentals=0
        ),
    )(where, *inputs)


def electron_sums(where, wk, own):
    return kernel_call(
        electron_kernel,
        where,
        (wk, own),
        [
            pl.BlockSpec((32, 32), lambda m, w: (0, 0)),
            pl.BlockSpec((16, 1, 2, 64, FIRST), lambda m, w: (0, (2 * w[0] + m) % 4, 0, 0, 0)),
        ],
        2,
        (2, 2, 2, 2, 8, 2, 2, 8, FIRST),
        (2, 1, 2, 2, 8, 1, 2, 8, FIRST),
        lambda m, w: (0, m // 2, 0, 0, 0, m % 2, 0, 0, 0),
        4,
        [pltpu.VMEM((256, 256), jnp.bfloat16), pltpu.VMEM((8, 32, 256), jnp.bfloat16)],
    )


def phonon_sums(where, wq, own, got):
    spec = pl.BlockSpec((2, 2, 8, 1, 2, 8, FIRST), lambda u, w: (0, 0, 0, u, 0, 0, 0))
    return kernel_call(
        phonon_kernel,
        where,
        (wq, own, got),
        [pl.BlockSpec((256, 256), lambda u, w: (0, 0)), spec, spec],
        2,
        (2, 2, 2, 2, 2, 2, 2, 8, FIRST),
        (2, 2, 2, 2, 2, 1, 2, 8, FIRST),
        lambda u, w: (0, 0, 0, 0, 0, u, 0, 0, 0),
        2,
        [pltpu.VMEM((2, 2, 2, 16, 8, FIRST), jnp.float32)],
    )


def own_spec(part, block_of):
    def place(t, w):
        mode, block = block_place(part, block_of(t))
        return (0, 2 * w[0] + mode, 0, 0, block)

    return pl.BlockSpec((16, 1, 2, 64, BLOCK), place)


def widened(part, where, own):
    def spec(blocks, mode):
        lanes = blocks * BLOCK
        at = 1 if blocks == 3 else 3
        return pl.BlockSpec((8, 1, 2, 64, lanes), lambda r, w: (r, 2 * (w[0] ^ 1) + mode, 0, 0, at))

    first = 0 if part == "x" else 1
    return kernel_call(
        lambda *refs: widen_kernel(part, *refs),
        where,
        (own, own),
        [spec(3, first), spec(2, 1 - first)],
        1,
        (16, 2, 64, BLOCKS * BLOCK),
        (8, 2, 64, BLOCKS * BLOCK),
        lambda r, w: (r, 0, 0, 0),
        2,
        [],
    )[0]


def partial_sums(part, where, wq, wk, own, got):
    return kernel_call(
        lambda *refs: partial_kernel(ORDER[part], *refs),
        where,
        (wq, wk, own, own, got),
        [
            pl.BlockSpec((256, 256), lambda t, w: (0, 0)),
            pl.BlockSpec((32, 32), lambda t, w: (0, 0)),
            own_spec(part, lambda t: 2 * t),
            own_spec(part, lambda t: jnp.minimum(2 * t + 1, BLOCKS - 1)),
            pl.BlockSpec((16, 2, 64, 2 * BLOCK), lambda t, w: (0, 0, 0, t)),
        ],
        2,
        (2, 2, 2, 2, 2, 2, 2, 2, 8, BLOCKS * BLOCK),
        (2, 2, 2, 2, 2, 2, 2, 2, 8, 2 * BLOCK),
        lambda t, w: (0, 0, 0, 0, 0, 0, 0, 0, 0, t),
        PAIRS,
        [
            pltpu.VMEM((16, 2, 16, 8, 2 * BLOCK), jnp.float32),
            pltpu.VMEM((2, 256, 256), jnp.bfloat16),
            pltpu.VMEM((8, 32, 256), jnp.bfloat16),
        ],
        vmem=57,
    )


def exchange(value, axis, step):
    pairs = []
    for core in range(2):
        for at in range(4):
            to = at ^ 1 if core == step else 3 - at
            if axis == "z":
                pairs.append((core * 4 + at, core * 4 + to))
            elif axis == "y":
                pairs.append((at * 2 + core, to * 2 + core))
            else:
                pairs.append(((at % 2) * 4 + core * 2 + at // 2, (to % 2) * 4 + core * 2 + to // 2))
    names = {"z": ("c", "z"), "y": ("y", "c"), "x": ("xl", "c", "xh")}[axis]
    return lax.ppermute(value, names, pairs)


def swap(value):
    return lax.ppermute(value, "c", [(0, 1), (1, 0)])


def rotation_tables(rot_right, rot_left):
    r_real, r_imag = (rot_right[:, 0], rot_right[:, 1])
    l_real, l_imag = (rot_left[:, :, 0], rot_left[:, :, 1])
    right = jnp.stack([jnp.stack([r_real, r_imag], 2), jnp.stack([-r_imag, r_real], 2)], 1)
    left = jnp.stack([jnp.stack([l_real, -l_imag], 3), jnp.stack([l_imag, l_real], 3)], 2)
    right = right.transpose(0, 1, 3, 2, 4)[:, :, :, None, :, None, :]
    right = right * jnp.eye(8, dtype=jnp.float32)[:, None, :, None]
    left = left.transpose(0, 1, 4, 5, 2, 3)
    return right.reshape(2, 2, 2, 256, 256), left.reshape(2, 8, 64, 64)


def split(value):
    high = value.astype(jnp.bfloat16)
    return high, (value - high.astype(jnp.float32)).astype(jnp.bfloat16)


def dot(left, right):
    return jnp.dot(left, right, preferred_element_type=jnp.float32)


def regroup(parts):
    group = lax.broadcasted_iota(jnp.int32, (8, 128), 1) // 32
    out = []
    for n in range(4):
        total = parts[n]
        for m in range(4):
            if m != n:
                total = jnp.where(group == m, pltpu.roll(parts[m], 32 * (m - n) % 128, 1), total)
        out.append(total)
    return out


def rotation_kernel(sum_ref, right_ref, left_ref, out_ref, turned_ref, done_ref):
    turned = [0.0, 0.0]
    for p in range(2):
        rows = sum_ref[0, p].reshape(32, 1024)
        rows = jnp.concatenate([rows[:, 256 * t : 256 * t + 256] for t in range(4)], axis=0)
        high, low = split(rows)
        both = jnp.concatenate([high, low], axis=0)
        for s in range(2):
            right_high, right_low = split(right_ref[0, p, s])
            product = dot(both, right_high)
            turned[s] = turned[s] + product[:128] + product[128:] + dot(high, right_low)
    for s in range(2):
        blocks = turned[s].reshape(4, 4, 8, 256)
        for t in range(8):
            parts = [blocks[t // 2, m, :, 128 * (t % 2) : 128 * (t % 2) + 128] for m in range(4)]
            for n, part in enumerate(regroup(parts)):
                spot = 8 * (32 * s + 4 * t + n)
                turned_ref[spot : spot + 8] = part
    for j in range(8):
        high, low = split(turned_ref[pl.ds(j, 64, stride=8), :])
        left_high, left_low = split(left_ref[0, j])
        product = dot(jnp.concatenate([left_high, left_low], axis=0), high)
        done_ref[pl.ds(j, 64, stride=8), :] = product[:64] + product[64:] + dot(left_high, low)
    for s in range(2):
        for t in range(8):
            spot = 8 * (32 * s + 4 * t)
            parts = [done_ref[spot + 8 * n : spot + 8 * n + 8] for n in range(4)]
            for m, part in enumerate(regroup(parts)):
                out_ref[0, :, m, s, 128 * t : 128 * t + 128] = part


def rotate(summed, right, left):
    return pl.pallas_call(
        rotation_kernel,
        grid=(2,),
        in_specs=[
            pl.BlockSpec((1, 2, 4, 8, 1024), lambda k: (k, 0, 0, 0, 0)),
            pl.BlockSpec((1, 2, 2, 256, 256), lambda k: (k, 0, 0, 0, 0)),
            pl.BlockSpec((1, 8, 64, 64), lambda k: (k, 0, 0, 0)),
        ],
        out_specs=pl.BlockSpec((1, 8, 4, 2, 1024), lambda k: (k, 0, 0, 0, 0)),
        out_shape=jax.ShapeDtypeStruct((2, 8, 4, 2, 1024), jnp.float32),
        scratch_shapes=[pltpu.VMEM((512, 128), jnp.float32)] * 2,
        compiler_params=pltpu.CompilerParams(vmem_limit_bytes=48 * 1024 * 1024),
        cost_estimate=pl.CostEstimate(flops=2**28, bytes_accessed=2**22, transcendentals=0),
    )(summed, right, left)


def complex_table(cos_part, sin_part):
    top = jnp.concatenate([cos_part, -sin_part], axis=1)
    bottom = jnp.concatenate([sin_part, cos_part], axis=1)
    return jnp.concatenate([top, bottom], axis=0)


def body(
    wannier_g, el_vectors, ph_vectors, el_degen, ph_degen, k_points, q_points, rot_right, rot_left
):
    core = lax.axis_index("c")
    where = jnp.stack([core, *(lax.axis_index(a) for a in ("y", "z", "xh", "xl"))]).astype(jnp.int32)

    vectors = jnp.concatenate([ph_vectors, ph_degen[None]], axis=0).astype(jnp.float32)
    others = swap(vectors)
    k_cos, k_sin = phase_table(k_points, el_vectors.astype(jnp.float32), el_degen.astype(jnp.float32))
    wide = jnp.stack([jnp.stack([k_cos, -k_sin], 2), jnp.stack([k_sin, k_cos], 2)], 1)
    wk = wide.reshape(32, 32)
    tables = [complex_table(*phase_table(q_points, v[:3], v[3])) for v in (vectors, others)]
    wq = jnp.concatenate(tables, axis=1)

    own = lax.optimization_barrier(wannier_g.transpose(0, 2, 3, 1, 4))

    def after(earlier, *values):
        return lax.optimization_barrier((*values, earlier))[:-1]

    keep, send, arrived = {}, {}, {}

    def begin(part, sums):
        keep[part], send[part] = sums
        arrived[part] = exchange(send[part], part, 0)

    (own,) = after(others, own)
    got_x = widened("x", where, own)
    (later,) = after(got_x, own)
    got_x = swap(got_x)
    got_y = widened("y", where, later)
    (wk,) = after(got_y, wk)
    got_y = swap(got_y)
    begin("z", electron_sums(where, wk, own))
    wq, got_x = after(keep["z"], wq, got_x)
    begin("x", partial_sums("x", where, wq, wk, own, got_x))
    wq, got_y = after(keep["x"], wq, got_y)
    begin("y", partial_sums("y", where, wq, wk, own, got_y))
    rot_right, rot_left = after(keep["y"], rot_right, rot_left)
    right, left = rotation_tables(rot_right, rot_left)
    latest = (right, left, keep["y"])
    for event in EVENTS:
        part, step = event
        axes = ORDER[part]
        (arrived[part],) = after(latest, arrived[part])
        if step == "0":
            latest = send[part] = keep[part][1] + arrived[part][1]
            held, came = after(latest, keep[part], arrived[part])
            arrived[part] = exchange(send[part], axes[0], 1)
            keep[part] = held[0] + came[0]
        elif step == "k":
            keep[part], send[part] = phonon_sums(where, wq, keep[part], arrived[part])
            arrived[part] = exchange(send[part], axes[1], 0)
            latest = keep[part]
        elif step == "5":
            latest = keep[part] = keep[part] + arrived[part]
        else:
            latest = send[part] = keep[part][1] + arrived[part][1]
            keep[part] = keep[part][0] + arrived[part][0]
            if event == "z1":
                arrived[part] = swap(send[part])
            else:
                arrived[part] = exchange(send[part], axes[(int(step) + 1) // 2], (int(step) + 1) % 2)

    modes = []
    for ours in (True, False):
        z, x, y = (keep[part][0] if ours else swap(keep[part][1]) for part in "zxy")
        wide, narrow = 3 * BLOCK, 2 * BLOCK
        modes.append(jnp.concatenate([z[:, 0], x[..., :wide], y[..., :narrow]], axis=-1))
        modes.append(jnp.concatenate([z[:, 1], y[..., narrow:], x[..., wide:]], axis=-1))
    mine, theirs = jnp.stack(modes[:2], axis=2), jnp.stack(modes[2:], axis=2)
    modes = jnp.concatenate([jnp.where(core == 0, mine, theirs), jnp.where(core == 0, theirs, mine)], axis=2)
    return rotate(modes, right, left)


def solution(mesh):
    fine = Mesh(mesh.devices.reshape(4, 2, 2, 2, 4), ("y", "xl", "c", "xh", "z"))
    ph, el = ("y", "xl", "c"), ("xh", "z")
    in_specs = (
        P(el, ph, None, None, None),
        P(None, el),
        P(None, ph),
        P(el),
        P(ph),
        P(),
        P(),
        P(el, None, None, None),
        P(el, ph, None, None, None),
    )
    out_specs = P(el, ph, None, None, None)
    return jax.shard_map(body, mesh=fine, in_specs=in_specs, out_specs=out_specs, check_vma=False)
```

```python
import itertools
import math

import jax
import jax.numpy as jnp
from jax import lax
from jax.experimental import pallas as pl
from jax.experimental.pallas import tpu as pltpu
from jax.sharding import Mesh, PartitionSpec as P

FIRST = 384
BLOCK = 128
BLOCKS = 5
PAIRS = 3
ORDER = {"z": "zxy", "x": "xyz", "y": "yzx"}
EVENTS = (
    *("z0", "x0", "y0", "z1", "x1", "zk"),
    *("y1", "x2", "z2", "y2", "x3", "z3"),
    *("x4", "y3", "z4", "x5", "y4", "z5", "y5"),
)


def block_place(part, t):
    if part == "x":
        return t // 3, t + 3
    return (t + 1) // 3, jnp.where(t < 2, t + 6, t + 1)


def phase_table(points, coords, degen):
    angle = points[0][:, None] * coords[0][None, :] + points[1][:, None] * coords[1][None, :]
    angle = angle + points[2][:, None] * coords[2][None, :]
    angle = 2.0 * jnp.pi * angle
    scale = 1.0 / degen
    return (
        (jnp.cos(angle) * scale[None, :]).astype(jnp.bfloat16),
        (jnp.sin(angle) * scale[None, :]).astype(jnp.bfloat16),
    )


def ring_place(place, core, first, second):
    high = place >> 1
    low = high ^ (place & 1)
    low = low ^ jnp.where(core == 0, first, second)
    high = high ^ jnp.where(core == 0, second, first)
    return 2 * high + (low ^ high)


def widen_kernel(part, where_ref, wide_ref, narrow_ref, out_ref):
    sources = (wide_ref, narrow_ref) if part == "x" else (narrow_ref, wide_ref)
    cut = sources[0].shape[-1]
    out_ref[..., :cut] = sources[0][:, 0].astype(jnp.float32)
    out_ref[..., cut:] = sources[1][:, 0].astype(jnp.float32)


def spread(table_ref, wide_ref):
    rows = lax.broadcasted_iota(jnp.int32, (256, 32), 0)
    entry = lax.broadcasted_iota(jnp.int32, (256, 32), 1)
    pick = (rows // 8 == entry).astype(jnp.float32).astype(jnp.bfloat16)
    table = jnp.dot(pick, table_ref[...], preferred_element_type=jnp.float32).astype(jnp.bfloat16)
    table = lax.dot_general(table, pick, (((1,), (1,)), ((), ())), preferred_element_type=jnp.float32)
    rows = lax.broadcasted_iota(jnp.int32, (256, 256), 0)
    entry = lax.broadcasted_iota(jnp.int32, (256, 256), 1)
    table = jnp.where(rows % 8 == entry % 8, table, 0.0).astype(jnp.bfloat16)
    wide_ref[...] = table.reshape(8, 32, 256)


def partial_kernel(order, where_ref, wq_ref, wk_ref, even_ref, odd_ref, got_ref, *refs):
    *out_refs, mixed_ref, rows_ref, wide_ref = refs
    core, y, z, xh, xl = (where_ref[n] for n in range(5))
    lanes = got_ref.shape[-1]

    @pl.when(pl.program_id(0) == 0)
    def _():
        spread(wk_ref, wide_ref)
        for h, zf, zs in itertools.product(range(2), repeat=3):
            zat = ring_place(z, core, zf, zs)
            spot = 32 * (4 * h + 2 * zf + zs)
            rows_ref[0, spot : spot + 32] = wide_ref[(xh ^ h) * 4 + zat]
            rows_ref[1, spot : spot + 32] = wide_ref[(xh ^ h ^ core) * 4 + zat]

    for r in range(16):
        even = even_ref[r, 0].reshape(128, BLOCK)
        odd = odd_ref[r, 0].reshape(128, BLOCK)
        own = jnp.concatenate([even, odd], axis=1)
        got = got_ref[r].reshape(128, lanes).astype(jnp.bfloat16)
        rows = jnp.concatenate([own, got], axis=0)
        mixed = jnp.dot(wq_ref[...], rows, preferred_element_type=jnp.float32)
        mixed_ref[r] = mixed.reshape(2, 16, 8, lanes)
    for yf, ys, cross, other in itertools.product(range(2), repeat=4):
        g = ring_place(y, core, yf, ys) * 4 + (xl ^ cross) * 2 + (core ^ other)
        rows = mixed_ref[:, :, g].reshape(256, lanes).astype(jnp.bfloat16)
        summed = jnp.dot(rows_ref[cross], rows, preferred_element_type=jnp.float32)
        summed = summed.reshape(2, 2, 2, 2, 2, 8, lanes)
        for h, zf, zs in itertools.product(range(2), repeat=3):
            bits = {"y": (yf, ys), "z": (zf, zs), "x": (h ^ cross, h)}
            spot = sum((bits[axis] for axis in order), ())
            out_refs[spot[0]][(*spot[1:], other)] = summed[h, zf, zs]


def electron_kernel(where_ref, wk_ref, own_ref, *refs):
    *out_refs, rows_ref, wide_ref = refs
    core, z, xh = (where_ref[n] for n in (0, 2, 3))
    lanes = own_ref.shape[-1]

    @pl.when(pl.program_id(0) == 0)
    def _():
        spread(wk_ref, wide_ref)
        for zf, zs, h in itertools.product(range(2), repeat=3):
            spot = 32 * (4 * zf + 2 * zs + h)
            rows_ref[spot : spot + 32] = wide_ref[(xh ^ h) * 4 + ring_place(z, core, zf, zs)]

    for pair in range(4):
        wide = own_ref[:, 0, :, 16 * pair : 16 * pair + 16].astype(jnp.float32)
        for half in range(2):
            rows = wide[:, :, 8 * half : 8 * half + 8].reshape(256, lanes).astype(jnp.bfloat16)
            summed = jnp.dot(rows_ref[...], rows, preferred_element_type=jnp.float32)
            summed = summed.reshape(2, 2, 2, 2, 2, 8, lanes)
            for n in range(2):
                out_refs[n][:, 0, :, :, 2 * pair + half, 0] = summed[n]


def phonon_kernel(where_ref, wq_ref, own_ref, got_ref, keep_ref, send_ref, summed_ref):
    core, y, xl = (where_ref[n] for n in (0, 1, 4))
    lanes = own_ref.shape[-1]
    for h, i in itertools.product(range(2), repeat=2):
        rows = [jnp.swapaxes(ref[h, i, :, 0], 0, 1).reshape(128, lanes) for ref in (own_ref, got_ref)]
        rows = jnp.concatenate(rows, axis=0).astype(jnp.bfloat16)
        summed = jnp.dot(wq_ref[...], rows, preferred_element_type=jnp.float32)
        summed_ref[h, i] = summed.reshape(2, 16, 8, lanes)
    for xf, xs in itertools.product(range(2), repeat=2):
        h = jnp.where(core == 0, xs, xf)
        for yf, ys, other in itertools.product(range(2), repeat=3):
            g = ring_place(y, core, yf, ys) * 4 + (xl ^ xf ^ xs) * 2 + (core ^ other)
            for i in range(2):
                (keep_ref, send_ref)[xf][xs, yf, ys, other, i, 0] = summed_ref[h, i, :, g]


def kernel_call(kernel, where, inputs, in_specs, count, out, block, place, grid, scratch, vmem=48):
    read = sum(v.size * v.dtype.itemsize for v in inputs)
    return pl.pallas_call(
        kernel,
        grid_spec=pltpu.PrefetchScalarGridSpec(
            num_scalar_prefetch=1,
            grid=(grid,),
            in_specs=in_specs,
            out_specs=[pl.BlockSpec(block, place)] * count,
            scratch_shapes=scratch,
        ),
        out_shape=[jax.ShapeDtypeStruct(out, jnp.float32)] * count,
        compiler_params=pltpu.CompilerParams(vmem_limit_bytes=vmem * 1024 * 1024),
        cost_estimate=pl.CostEstimate(
            flops=2**31, bytes_accessed=read + 4 * count * math.prod(out), transcendentals=0
        ),
    )(where, *inputs)


def electron_sums(where, wk, own):
    return kernel_call(
        electron_kernel,
        where,
        (wk, own),
        [
            pl.BlockSpec((32, 32), lambda m, w: (0, 0)),
            pl.BlockSpec((16, 1, 2, 64, FIRST), lambda m, w: (0, (2 * w[0] + m) % 4, 0, 0, 0)),
        ],
        2,
        (2, 2, 2, 2, 8, 2, 2, 8, FIRST),
        (2, 1, 2, 2, 8, 1, 2, 8, FIRST),
        lambda m, w: (0, m // 2, 0, 0, 0, m % 2, 0, 0, 0),
        4,
        [pltpu.VMEM((256, 256), jnp.bfloat16), pltpu.VMEM((8, 32, 256), jnp.bfloat16)],
    )


def phonon_sums(where, wq, own, got):
    spec = pl.BlockSpec((2, 2, 8, 1, 2, 8, FIRST), lambda u, w: (0, 0, 0, u, 0, 0, 0))
    return kernel_call(
        phonon_kernel,
        where,
        (wq, own, got),
        [pl.BlockSpec((256, 256), lambda u, w: (0, 0)), spec, spec],
        2,
        (2, 2, 2, 2, 2, 2, 2, 8, FIRST),
        (2, 2, 2, 2, 2, 1, 2, 8, FIRST),
        lambda u, w: (0, 0, 0, 0, 0, u, 0, 0, 0),
        2,
        [pltpu.VMEM((2, 2, 2, 16, 8, FIRST), jnp.float32)],
    )


def own_spec(part, block_of):
    def place(t, w):
        mode, block = block_place(part, block_of(t))
        return (0, 2 * w[0] + mode, 0, 0, block)

    return pl.BlockSpec((16, 1, 2, 64, BLOCK), place)


def widened(part, where, own):
    def spec(blocks, mode):
        lanes = blocks * BLOCK
        at = 1 if blocks == 3 else 3
        return pl.BlockSpec((8, 1, 2, 64, lanes), lambda r, w: (r, 2 * (w[0] ^ 1) + mode, 0, 0, at))

    first = 0 if part == "x" else 1
    return kernel_call(
        lambda *refs: widen_kernel(part, *refs),
        where,
        (own, own),
        [spec(3, first), spec(2, 1 - first)],
        1,
        (16, 2, 64, BLOCKS * BLOCK),
        (8, 2, 64, BLOCKS * BLOCK),
        lambda r, w: (r, 0, 0, 0),
        2,
        [],
    )[0]


def partial_sums(part, where, wq, wk, own, got):
    return kernel_call(
        lambda *refs: partial_kernel(ORDER[part], *refs),
        where,
        (wq, wk, own, own, got),
        [
            pl.BlockSpec((256, 256), lambda t, w: (0, 0)),
            pl.BlockSpec((32, 32), lambda t, w: (0, 0)),
            own_spec(part, lambda t: 2 * t),
            own_spec(part, lambda t: jnp.minimum(2 * t + 1, BLOCKS - 1)),
            pl.BlockSpec((16, 2, 64, 2 * BLOCK), lambda t, w: (0, 0, 0, t)),
        ],
        2,
        (2, 2, 2, 2, 2, 2, 2, 2, 8, BLOCKS * BLOCK),
        (2, 2, 2, 2, 2, 2, 2, 2, 8, 2 * BLOCK),
        lambda t, w: (0, 0, 0, 0, 0, 0, 0, 0, 0, t),
        PAIRS,
        [
            pltpu.VMEM((16, 2, 16, 8, 2 * BLOCK), jnp.float32),
            pltpu.VMEM((2, 256, 256), jnp.bfloat16),
            pltpu.VMEM((8, 32, 256), jnp.bfloat16),
        ],
        vmem=57,
    )


def exchange(value, axis, step):
    pairs = []
    for core in range(2):
        for at in range(4):
            to = at ^ 1 if core == step else 3 - at
            if axis == "z":
                pairs.append((core * 4 + at, core * 4 + to))
            elif axis == "y":
                pairs.append((at * 2 + core, to * 2 + core))
            else:
                pairs.append(((at % 2) * 4 + core * 2 + at // 2, (to % 2) * 4 + core * 2 + to // 2))
    names = {"z": ("c", "z"), "y": ("y", "c"), "x": ("xl", "c", "xh")}[axis]
    return lax.ppermute(value, names, pairs)


def swap(value):
    return lax.ppermute(value, "c", [(0, 1), (1, 0)])


def rotation_tables(rot_right, rot_left):
    r_real, r_imag = (rot_right[:, 0], rot_right[:, 1])
    l_real, l_imag = (rot_left[:, :, 0], rot_left[:, :, 1])
    right = jnp.stack([jnp.stack([r_real, r_imag], 2), jnp.stack([-r_imag, r_real], 2)], 1)
    left = jnp.stack([jnp.stack([l_real, -l_imag], 3), jnp.stack([l_imag, l_real], 3)], 2)
    right = right.transpose(0, 1, 3, 2, 4)[:, :, :, None, :, None, :]
    right = right * jnp.eye(8, dtype=jnp.float32)[:, None, :, None]
    left = left.transpose(0, 1, 4, 5, 2, 3)
    return right.reshape(2, 2, 2, 256, 256), left.reshape(2, 8, 64, 64)


def split(value):
    high = value.astype(jnp.bfloat16)
    return high, (value - high.astype(jnp.float32)).astype(jnp.bfloat16)


def dot(left, right):
    return jnp.dot(left, right, preferred_element_type=jnp.float32)


def regroup(parts):
    group = lax.broadcasted_iota(jnp.int32, (8, 128), 1) // 32
    out = []
    for n in range(4):
        total = parts[n]
        for m in range(4):
            if m != n:
                total = jnp.where(group == m, pltpu.roll(parts[m], 32 * (m - n) % 128, 1), total)
        out.append(total)
    return out


def rotation_kernel(sum_ref, right_ref, left_ref, out_ref, turned_ref, done_ref):
    turned = [0.0, 0.0]
    for p in range(2):
        rows = sum_ref[0, p].reshape(32, 1024)
        rows = jnp.concatenate([rows[:, 256 * t : 256 * t + 256] for t in range(4)], axis=0)
        high, low = split(rows)
        both = jnp.concatenate([high, low], axis=0)
        for s in range(2):
            right_high, right_low = split(right_ref[0, p, s])
            product = dot(both, right_high)
            turned[s] = turned[s] + product[:128] + product[128:] + dot(high, right_low)
    for s in range(2):
        blocks = turned[s].reshape(4, 4, 8, 256)
        for t in range(8):
            parts = [blocks[t // 2, m, :, 128 * (t % 2) : 128 * (t % 2) + 128] for m in range(4)]
            for n, part in enumerate(regroup(parts)):
                spot = 8 * (32 * s + 4 * t + n)
                turned_ref[spot : spot + 8] = part
    for j in range(8):
        high, low = split(turned_ref[pl.ds(j, 64, stride=8), :])
        left_high, left_low = split(left_ref[0, j])
        product = dot(jnp.concatenate([left_high, left_low], axis=0), high)
        done_ref[pl.ds(j, 64, stride=8), :] = product[:64] + product[64:] + dot(left_high, low)
    for s in range(2):
        for t in range(8):
            spot = 8 * (32 * s + 4 * t)
            parts = [done_ref[spot + 8 * n : spot + 8 * n + 8] for n in range(4)]
            for m, part in enumerate(regroup(parts)):
                out_ref[0, :, m, s, 128 * t : 128 * t + 128] = part


def rotate(summed, right, left):
    return pl.pallas_call(
        rotation_kernel,
        grid=(2,),
        in_specs=[
            pl.BlockSpec((1, 2, 4, 8, 1024), lambda k: (k, 0, 0, 0, 0)),
            pl.BlockSpec((1, 2, 2, 256, 256), lambda k: (k, 0, 0, 0, 0)),
            pl.BlockSpec((1, 8, 64, 64), lambda k: (k, 0, 0, 0)),
        ],
        out_specs=pl.BlockSpec((1, 8, 4, 2, 1024), lambda k: (k, 0, 0, 0, 0)),
        out_shape=jax.ShapeDtypeStruct((2, 8, 4, 2, 1024), jnp.float32),
        scratch_shapes=[pltpu.VMEM((512, 128), jnp.float32)] * 2,
        compiler_params=pltpu.CompilerParams(vmem_limit_bytes=48 * 1024 * 1024),
        cost_estimate=pl.CostEstimate(flops=2**28, bytes_accessed=2**22, transcendentals=0),
    )(summed, right, left)


def complex_table(cos_part, sin_part):
    top = jnp.concatenate([cos_part, -sin_part], axis=1)
    bottom = jnp.concatenate([sin_part, cos_part], axis=1)
    return jnp.concatenate([top, bottom], axis=0)


def body(
    wannier_g, el_vectors, ph_vectors, el_degen, ph_degen, k_points, q_points, rot_right, rot_left
):
    core = lax.axis_index("c")
    where = jnp.stack([core, *(lax.axis_index(a) for a in ("y", "z", "xh", "xl"))]).astype(jnp.int32)

    vectors = jnp.concatenate([ph_vectors, ph_degen[None]], axis=0).astype(jnp.float32)
    others = swap(vectors)
    k_cos, k_sin = phase_table(k_points, el_vectors.astype(jnp.float32), el_degen.astype(jnp.float32))
    wide = jnp.stack([jnp.stack([k_cos, -k_sin], 2), jnp.stack([k_sin, k_cos], 2)], 1)
    wk = wide.reshape(32, 32)
    tables = [complex_table(*phase_table(q_points, v[:3], v[3])) for v in (vectors, others)]
    wq = jnp.concatenate(tables, axis=1)

    own = lax.optimization_barrier(wannier_g.transpose(0, 2, 3, 1, 4))

    def after(earlier, *values):
        return lax.optimization_barrier((*values, earlier))[:-1]

    keep, send, arrived = {}, {}, {}

    def begin(part, sums):
        keep[part], send[part] = sums
        arrived[part] = exchange(send[part], part, 0)

    (own,) = after(others, own)
    got_x = widened("x", where, own)
    (later,) = after(got_x, own)
    got_x = swap(got_x)
    got_y = widened("y", where, later)
    (wk,) = after(got_y, wk)
    got_y = swap(got_y)
    begin("z", electron_sums(where, wk, own))
    wq, got_x = after(keep["z"], wq, got_x)
    begin("x", partial_sums("x", where, wq, wk, own, got_x))
    wq, got_y = after(keep["x"], wq, got_y)
    begin("y", partial_sums("y", where, wq, wk, own, got_y))
    rot_right, rot_left = after(keep["y"], rot_right, rot_left)
    right, left = rotation_tables(rot_right, rot_left)
    latest = (right, left, keep["y"])
    for event in EVENTS:
        part, step = event
        axes = ORDER[part]
        (arrived[part],) = after(latest, arrived[part])
        if step == "0":
            latest = send[part] = keep[part][1] + arrived[part][1]
            held, came = after(latest, keep[part], arrived[part])
            arrived[part] = exchange(send[part], axes[0], 1)
            keep[part] = held[0] + came[0]
        elif step == "k":
            keep[part], send[part] = phonon_sums(where, wq, keep[part], arrived[part])
            arrived[part] = exchange(send[part], axes[1], 0)
            latest = keep[part]
        elif step == "5":
            latest = keep[part] = keep[part] + arrived[part]
        else:
            latest = send[part] = keep[part][1] + arrived[part][1]
            keep[part] = keep[part][0] + arrived[part][0]
            if event == "z1":
                arrived[part] = swap(send[part])
            else:
                arrived[part] = exchange(send[part], axes[(int(step) + 1) // 2], (int(step) + 1) % 2)

    modes = []
    for ours in (True, False):
        z, x, y = (keep[part][0] if ours else swap(keep[part][1]) for part in "zxy")
        wide, narrow = 3 * BLOCK, 2 * BLOCK
        modes.append(jnp.concatenate([z[:, 0], x[..., :wide], y[..., :narrow]], axis=-1))
        modes.append(jnp.concatenate([z[:, 1], y[..., narrow:], x[..., wide:]], axis=-1))
    mine, theirs = jnp.stack(modes[:2], axis=2), jnp.stack(modes[2:], axis=2)
    modes = jnp.concatenate([jnp.where(core == 0, mine, theirs), jnp.where(core == 0, theirs, mine)], axis=2)
    return rotate(modes, right, left)


def solution(mesh):
    fine = Mesh(mesh.devices.reshape(4, 2, 2, 2, 4), ("y", "xl", "c", "xh", "z"))
    ph, el = ("y", "xl", "c"), ("xh", "z")
    in_specs = (
        P(el, ph, None, None, None),
        P(None, el),
        P(None, ph),
        P(el),
        P(ph),
        P(),
        P(),
        P(el, None, None, None),
        P(el, ph, None, None, None),
    )
    out_specs = P(el, ph, None, None, None)
    return jax.shard_map(body, mesh=fine, in_specs=in_specs, out_specs=out_specs, check_vma=False)
```
